32 devices in a mesh: section: 4 (over y, core), dp: 8 (over z, x).
Axes of the slice: x: 2, y: 2, z: 4, core: 2. Of those that a mesh axis runs over, the one named last changes fastest.
Arguments:
- tokens: bfloat16 [128, 56, 768], P(('section', 'dp')), may hold values from -6 to 6
- cotangent: bfloat16 [128, 56, 768], P(('section', 'dp')), may hold values from -6 to 6
- task_flags: int32 [128], P(('section', 'dp')), may hold values from 0 to 2
- w_query: bfloat16 [4, 768, 768], P('section'), may hold values from -0.21875 to 0.21875
- w_key: bfloat16 [4, 768, 768], P('section'), may hold values from -0.21875 to 0.21875
- w_value: bfloat16 [4, 768, 768], P('section'), may hold values from -0.21875 to 0.21875
- w_attn_out: bfloat16 [4, 768, 768], P('section'), may hold values from -0.5 to 0.5
- b_query: bfloat16 [4, 768], P('section'), may hold values from -2 to 2
- b_value: bfloat16 [4, 768], P('section'), may hold values from -2 to 2
- b_attn_out: bfloat16 [4, 768], P('section'), may hold values from -2 to 2
- norm1_gain: bfloat16 [4, 768], P('section'), may hold values from 0.25 to 1.75
- norm1_bias: bfloat16 [4, 768], P('section'), may hold values from -1.5 to 1.5
- w_inner: bfloat16 [4, 768, 3072], P('section'), may hold values from -0.21875 to 0.21875
- b_inner: bfloat16 [4, 3072], P('section'), may hold values from -2 to 2
- w_outer: bfloat16 [4, 3072, 768], P('section'), may hold values from -0.109375 to 0.109375
- b_outer: bfloat16 [4, 768], P('section'), may hold values from -2 to 2
- norm2_gain: bfloat16 [4, 768], P('section'), may hold values from 0.25 to 1.75
- norm2_bias: bfloat16 [4, 768], P('section'), may hold values from -1.5 to 1.5
Outputs:
- mixed: bfloat16 [128, 56, 768], P(('section', 'dp'))
- tokens_grad: bfloat16 [128, 56, 768], P(('section', 'dp'))
- grad_w_query: float32 [4, 768, 768], P('section')
- grad_w_key: float32 [4, 768, 768], P('section')
- grad_w_value: float32 [4, 768, 768], P('section')
- grad_w_attn_out: float32 [4, 768, 768], P('section')
- grad_b_query: float32 [4, 768], P('section')
- grad_b_value: float32 [4, 768], P('section')
- grad_b_attn_out: float32 [4, 768], P('section')
- grad_norm1_gain: float32 [4, 768], P('section')
- grad_norm1_bias: float32 [4, 768], P('section')
- grad_w_inner: float32 [4, 768, 3072], P('section')
- grad_b_inner: float32 [4, 3072], P('section')
- grad_w_outer: float32 [4, 3072, 768], P('section')
- grad_b_outer: float32 [4, 768], P('section')
- grad_norm2_gain: float32 [4, 768], P('section')
- grad_norm2_bias: float32 [4, 768], P('section')
The draws below stay inside these ranges and needn't reach their ends.
All inputs are finite; a program needn't handle non-finite values.
Results may differ from the reference program's by a relative error of at most 0.025.
Values may be sent and summed in bfloat16 or wider, within the bound.
No kernel may reach another device: no remote copies, remote signals or barrier semaphores. Data moves between devices by JAX's collectives and lax.ppermute only.
A program may use at most 768 MiB of HBM per device.

```python
import jax
import jax.numpy as jnp
from jax import lax

D = 768
HEADS = 12
HEAD_DIM = 64
FF = 3072
OBJ = 36
SEQ = 56
MB = 4
IMB = 4
ITEMS = 128
SECTIONS = 4
N_SECTION = 4


def place_ends(result, key, least, top_value):
    longest = result.shape.index(max(result.shape))
    spots = []
    for shift in (0, 1):
        where = [jax.random.randint(jax.random.fold_in(key, axis), (), 0, length) for axis, length in enumerate(result.shape)]
        where[longest] = (where[longest] + shift) % result.shape[longest]
        spots.append(tuple(where))
    return result.at[spots[0]].set(least).at[spots[1]].set(top_value)


def levels(rng, shape, cuts, smallest, top_value):
    level, own = 1.0, jax.random.fold_in(rng, 6)
    for dim, blocks in cuts:
        heights = jnp.exp(jax.random.uniform(jax.random.fold_in(own, dim), (blocks,), jnp.float32, smallest / len(cuts), top_value / len(cuts)))
        level = level * jnp.repeat(heights, shape[dim] // blocks).reshape([-1 if axis == dim else 1 for axis in range(len(shape))])
    return level


def normal_values(own_key, dims, spread, reach, cuts=(), kind=jnp.bfloat16):
    entries = spread * jax.random.normal(own_key, dims, jnp.float32)
    if cuts:
        entries = entries * levels(own_key, dims, cuts, -0.22, 0.18)
    return jnp.clip(entries, -reach, reach).astype(kind)


def setup_inputs(seed: int = 0) -> dict:
    keys = jax.random.split(jax.random.key(seed), 19)
    return {
        "tokens": normal_values(keys[0], (ITEMS, SEQ, D), 1.0, 6.0, ((0, 32),)),
        "cotangent": normal_values(keys[1], (ITEMS, SEQ, D), 1.0, 6.0, ((0, 32),)),
        "task_flags": place_ends(jax.random.randint(keys[2], (ITEMS,), 0, 3), jax.random.fold_in(keys[2], 1), 0, 2).astype(jnp.int32),
        "w_query": normal_values(keys[3], (SECTIONS, D, D), D ** -0.5, 0.21875, ((0, 4),)),
        "w_key": normal_values(keys[4], (SECTIONS, D, D), D ** -0.5, 0.21875, ((0, 4),)),
        "w_value": normal_values(keys[5], (SECTIONS, D, D), D ** -0.5, 0.21875, ((0, 4),)),
        "w_attn_out": normal_values(keys[6], (SECTIONS, D, D), (D // 6) ** -0.5, 0.5, ((0, 4),)),
        "b_query": normal_values(keys[7], (SECTIONS, D), 0.4, 2.0, ((0, 4),)),
        "b_value": normal_values(keys[8], (SECTIONS, D), 0.4, 2.0, ((0, 4),)),
        "b_attn_out": normal_values(keys[9], (SECTIONS, D), 0.4, 2.0, ((0, 4),)),
        "norm1_gain": jnp.clip(1.0 + 0.15 * jax.random.normal(keys[10], (SECTIONS, D), jnp.float32), 0.25, 1.75).astype(jnp.bfloat16),
        "norm1_bias": normal_values(keys[11], (SECTIONS, D), 0.3, 1.5, ((0, 4),)),
        "w_inner": normal_values(keys[12], (SECTIONS, D, FF), D ** -0.5, 0.21875, ((0, 4),)),
        "b_inner": normal_values(keys[13], (SECTIONS, FF), 0.4, 2.0, ((0, 4),)),
        "w_outer": normal_values(keys[14], (SECTIONS, FF, D), FF ** -0.5, 0.109375, ((0, 4),)),
        "b_outer": normal_values(keys[15], (SECTIONS, D), 0.4, 2.0, ((0, 4),)),
        "norm2_gain": jnp.clip(1.0 + 0.15 * jax.random.normal(keys[16], (SECTIONS, D), jnp.float32), 0.25, 1.75).astype(jnp.bfloat16),
        "norm2_bias": normal_values(keys[17], (SECTIONS, D), 0.3, 1.5, ((0, 4),)),
    }


EPS = 1e-06
NEG = -1000000000.0

@jax.custom_vjp
def low(v):
    return lax.optimization_barrier(v.astype(jnp.bfloat16)).astype(jnp.float32)

@jax.custom_vjp
def low_back(v):
    return v

def low_keep(v):
    return (low(v), None)

def low_pass(kept, grad):
    return (grad,)

def back_keep(v):
    return (v, None)

def back_low(kept, grad):
    return (low(grad),)
low.defvjp(low_keep, low_pass)
low_back.defvjp(back_keep, back_low)

def rounded_both(value):
    return low(low_back(value))

def project(inputs, matrix):
    return jnp.matmul(inputs, matrix, precision=lax.Precision.HIGHEST)

def layer_norm(values, gain, bias):
    centered = values - lax.optimization_barrier(jnp.mean(values, -1, keepdims=True))
    variance = lax.optimization_barrier(jnp.mean(centered * centered, -1, keepdims=True))
    return centered * lax.rsqrt(variance + EPS) * gain + bias

def section_masks(section, seq_len):
    position = jnp.arange(seq_len)
    visual = position < OBJ
    wanted = visual == (section != 3)
    crossing = section == 1
    key_mask = jnp.where(crossing, visual[:, None] != visual[None, :], jnp.logical_and(visual[:, None] == visual[None, :], wanted[:, None]))
    attn_rows = jnp.logical_or(crossing, wanted)
    ffn_rows = jnp.logical_and(jnp.logical_not(crossing), wanted)
    return (key_mask, attn_rows, ffn_rows)

def section_forward(section, inputs, head_used, weights):
    w_query, w_key, w_value, w_attn_out, b_query, b_value, b_attn_out, norm1_gain, norm1_bias, w_inner, b_inner, w_outer, b_outer, norm2_gain, norm2_bias = weights
    items = inputs.shape[0]
    key_mask, attn_rows, ffn_rows = section_masks(section, SEQ)
    split = (items, SEQ, HEADS, HEAD_DIM)
    queries = rounded_both(project(inputs, w_query) + b_query).reshape(split)
    key_rows = rounded_both(project(inputs, w_key)).reshape(split)
    values = rounded_both(project(inputs, w_value) + b_value).reshape(split)
    scores = low_back(jnp.einsum('nihd,njhd->nhij', queries, key_rows, precision=lax.Precision.HIGHEST) * HEAD_DIM ** (-0.5))
    scores = jnp.where(key_mask, scores, NEG)
    shifted = jnp.exp(scores - lax.optimization_barrier(jnp.max(scores, -1, keepdims=True)))
    probs = shifted / lax.optimization_barrier(jnp.sum(shifted, -1, keepdims=True))
    context = jnp.einsum('nhij,njhd->nihd', low(probs), values, precision=lax.Precision.HIGHEST) * head_used[:, None, :, None]
    context = rounded_both(context).reshape(items, SEQ, D)
    attn_out = low_back(project(context, w_attn_out) + b_attn_out)
    middle = jnp.where(attn_rows[:, None], layer_norm(inputs + attn_out, norm1_gain, norm1_bias), inputs)
    inner = low_back(project(low(middle), w_inner) + b_inner)
    outer = low_back(project(low(jax.nn.gelu(inner, approximate=False)), w_outer) + b_outer)
    return jnp.where(ffn_rows[:, None], layer_norm(middle + outer, norm2_gain, norm2_bias), middle)

def reference(tokens, cotangent, task_flags, w_query, w_key, w_value, w_attn_out, b_query, b_value, b_attn_out, norm1_gain, norm1_bias, w_inner, b_inner, w_outer, b_outer, norm2_gain, norm2_bias):
    weights = tuple((w.astype(jnp.float32) for w in (w_query, w_key, w_value, w_attn_out, b_query, b_value, b_attn_out, norm1_gain, norm1_bias, w_inner, b_inner, w_outer, b_outer, norm2_gain, norm2_bias)))
    head_used = (jnp.arange(HEADS)[None, :] % 3 != task_flags[:, None]).astype(jnp.float32)
    group_items = MB * IMB
    groups = ITEMS // group_items

    def forward(params, inputs):

        def group_pass(pieces):
            current, heads_on = pieces
            current = rounded_both(current)
            for section in range(N_SECTION):
                section_weights = tuple((w[section] for w in params))
                current = rounded_both(section_forward(section, current, heads_on, section_weights))
            return current
        outputs = lax.map(jax.checkpoint(group_pass), (inputs.reshape(groups, group_items, SEQ, D), head_used.reshape(groups, group_items, HEADS)))
        return outputs.reshape(ITEMS, SEQ, D)
    mixed, pull = jax.vjp(forward, weights, tokens.astype(jnp.float32))
    grads, token_grads = pull(cotangent.astype(jnp.float32))
    return (mixed.astype(jnp.bfloat16), token_grads.astype(jnp.bfloat16), grads[0], grads[1], grads[2], grads[3], grads[4], grads[5], grads[6], grads[7], grads[8], grads[9], grads[10], grads[11], grads[12], grads[13], grads[14])
```

```python
import jax
import jax.numpy as jnp
from jax import lax
from jax.experimental import pallas as pl
from jax.experimental.pallas import tpu as pltpu
from jax.sharding import PartitionSpec as P

HEADS = 12
HEAD_DIM = 64
OBJ = 36
PAIRS = HEADS // 2
EPS = 1e-06
NEG = -1000000000.0
F32 = jnp.float32
BF16 = jnp.bfloat16
LANES = 128
BLOCKS = 4
EXTRA = 32
VMEM = 60 * 1024 * 1024


def mm(a, b):
    return jnp.dot(a, b, preferred_element_type=F32)


def mm_nt(a, b):
    return lax.dot_general(a, b, (((1,), (1,)), ((), ())), preferred_element_type=F32)


def mm_tn(a, b):
    return lax.dot_general(a, b, (((0,), (0,)), ((), ())), preferred_element_type=F32)


def each_rows(count, step, body):
    def turn(i, carry):
        body(pl.ds(pl.multiple_of(i * step, step), step))
        return carry

    lax.fori_loop(0, count // step, turn, 0)


def folded(values):
    rows, width = values.shape
    return jnp.sum(values.reshape(rows // 8, 8, width), 0)


class Copies:
    def __init__(self, sems):
        self.sems, self.used, self.stores = sems, 0, []

    def next_sem(self):
        self.used += 1
        return self.sems.at[self.used - 1]

    def load(self, source, target):
        copy = pltpu.make_async_copy(source, target, self.next_sem())
        copy.start()
        return copy

    def load_either(self, first, own, other, target):
        sem = self.next_sem()
        mine = pltpu.make_async_copy(own, target, sem)

        @pl.when(first)
        def _():
            mine.start()

        @pl.when(jnp.logical_not(first))
        def _():
            pltpu.make_async_copy(other, target, sem).start()

        return mine

    def store(self, source, target):
        copy = pltpu.make_async_copy(source, target, self.next_sem())
        copy.start()
        self.stores.append(copy)

    def store_either(self, first, source, target, other):
        sem = self.next_sem()
        mine = pltpu.make_async_copy(source, target, sem)

        @pl.when(first)
        def _():
            mine.start()

        @pl.when(jnp.logical_not(first))
        def _():
            pltpu.make_async_copy(source, other, sem).start()

        self.stores.append(mine)

    def drain(self):
        for copy in self.stores:
            copy.wait()
        self.stores = []


def kernel_call(
    body, control, inputs, outs, scratch, sems, flops, moved, name, aliases=None, with_block=False
):
    n_in, n_out = len(inputs), len(outs)

    def kernel(control_ref, *refs):
        @pl.when(control_ref[0] == 1)
        def _():
            body(
                control_ref[1] == 1,
                *([control_ref[2]] if with_block else []),
                refs[:n_in],
                refs[n_in : n_in + n_out],
                refs[n_in + n_out : -1],
                Copies(refs[-1]),
            )

    return pl.pallas_call(
        kernel,
        out_shape=[jax.ShapeDtypeStruct(shape, kind) for shape, kind in outs],
        in_specs=[pl.BlockSpec(memory_space=pltpu.SMEM)]
        + [pl.BlockSpec(memory_space=pl.ANY)] * n_in,
        out_specs=[pl.BlockSpec(memory_space=pl.ANY)] * n_out,
        scratch_shapes=[pltpu.VMEM(shape, kind) for shape, kind in scratch]
        + [pltpu.SemaphoreType.DMA((sems,))],
        input_output_aliases=aliases or {},
        compiler_params=pltpu.CompilerParams(vmem_limit_bytes=VMEM),
        cost_estimate=pl.CostEstimate(flops=flops, bytes_accessed=moved, transcendentals=0),
        name=name,
    )(control, *inputs)


def norm_stats(values):
    centered = values - jnp.mean(values, -1, keepdims=True)
    inverse = lax.rsqrt(jnp.mean(centered * centered, -1, keepdims=True) + EPS)
    return centered * inverse, inverse


def norm_back(grad_out, normed, inverse, gain):
    scaled = grad_out * gain
    return inverse * (
        scaled
        - jnp.mean(scaled, -1, keepdims=True)
        - normed * jnp.mean(scaled * normed, -1, keepdims=True)
    )


def head_keep(pair, flags):
    lane = lax.broadcasted_iota(jnp.int32, flags.shape, 1)
    head = 2 * pair + jnp.where(lane >= HEAD_DIM, 1, 0)
    return jnp.where(lax.rem(head, 3).astype(F32) != flags, 1.0, 0.0)


def half_masks(rows):
    lane = lax.broadcasted_iota(jnp.int32, (rows, LANES), 1)
    low = jnp.where(lane < HEAD_DIM, 1.0, 0.0)
    return low.astype(BF16), (1.0 - low).astype(BF16), lane < HEAD_DIM


def stacked_halves(piece, low, high):
    return jnp.concatenate([piece * low, piece * high], 0)


def attn_forward(control, xs, flags, vecs, weights, blocks, final, name):
    rows = sum(x.shape[0] for x in xs)
    width = xs[0].shape[1]
    probs_shapes = [((PAIRS, 2 * nq, nk), BF16) for _, nq, _, _, nk, _ in blocks]
    narrow, wide = ((rows, width), BF16), ((rows, width), F32)
    tails = [((x.shape[0], width), BF16) for x in xs] if final else [wide, narrow]
    n_x, n_b, n_t = len(xs), len(blocks), len(tails)
    n_rest = 4

    def body(first, ins, outs, scr, copies):
        x_in, flags_in, vec_in, w_in = ins[:n_x], ins[n_x], ins[n_x + 1 : n_x + 3], ins[n_x + 3 :]
        x_s, flags_s, vec_s, w_s, q_s, k_s, v_s, ctx_s, before_s, tail_s = scr[:10]
        probs_s = scr[10:]
        at, x_loads = 0, []
        for piece in x_in:
            x_loads.append(copies.load(piece, x_s.at[pl.ds(at, piece.shape[0])]))
            at += piece.shape[0]
        vec_load = copies.load_either(first, vec_in[0], vec_in[1], vec_s)
        w_loads = [
            copies.load_either(first, w_in[2 * i], w_in[2 * i + 1], w_s.at[i]) for i in range(4)
        ]
        flags_load = copies.load(flags_in, flags_s)
        for load in x_loads:
            load.wait()
        vec_load.wait()
        vec = vec_s[...].astype(F32)
        for i, (target, bias) in enumerate(((q_s, 0), (k_s, None), (v_s, 1))):
            w_loads[i].wait()
            product = mm(x_s[...], w_s[i])
            if bias is not None:
                product = product + vec[bias : bias + 1]
            target[...] = product.astype(BF16)
        copies.store(q_s, outs[0])
        copies.store(k_s, outs[1])
        copies.store(v_s, outs[2])
        flags_load.wait()
        for index, (q0, nq, iq, k0, nk, ik) in enumerate(blocks):
            low, high, is_low = half_masks(nq)
            row = lax.broadcasted_iota(jnp.int32, (nq, nk), 0) // iq
            col = lax.broadcasted_iota(jnp.int32, (nq, nk), 1) // ik
            same = jnp.where(row == col, 0.0, 1.0)
            same = jnp.concatenate([same, same], 0)

            def pair_turn(pair, carry):
                lanes = pl.ds(pl.multiple_of(pair * LANES, LANES), LANES)
                q2 = stacked_halves(q_s[pl.ds(q0, nq), lanes], low, high)
                scores = mm_nt(q2, k_s[pl.ds(k0, nk), lanes]) * (HEAD_DIM ** (-0.5))
                scores = jnp.where(same > 0.0, NEG, scores)
                shifted = jnp.exp(scores - jnp.max(scores, -1, keepdims=True))
                probs = (shifted / jnp.sum(shifted, -1, keepdims=True)).astype(BF16)
                probs_s[index][pair] = probs
                mixed = mm(probs, v_s[pl.ds(k0, nk), lanes])
                keep = head_keep(pair, flags_s[pl.ds(q0, nq), :])
                ctx = jnp.where(is_low, mixed[:nq], mixed[nq:]) * keep
                ctx_s[pl.ds(q0, nq), lanes] = ctx.astype(BF16)
                return carry

            lax.fori_loop(0, PAIRS, pair_turn, 0, unroll=2)
            copies.store(probs_s[index], outs[5 + index])
        copies.store(ctx_s, outs[3])
        w_loads[3].wait()
        before_s[...] = mm(ctx_s[...], w_s[3])

        def finish(where):
            before = x_s[where, :].astype(F32) + (before_s[where, :] + vec[2:3])
            before_s[where, :] = before
            normed, _ = norm_stats(before)
            middle = normed * vec[3:4] + vec[4:5]
            tail_s[where, :] = middle.astype(tail_s.dtype)
            if not final:
                q_s[where, :] = middle.astype(BF16)

        if not final:
            copies.drain()
        each_rows(rows, 32, finish)
        copies.store(before_s, outs[4])
        if final:
            at = 0
            for target in outs[5 + n_b :]:
                copies.store(tail_s.at[pl.ds(at, target.shape[0])], target)
                at += target.shape[0]
        else:
            copies.store(tail_s, outs[5 + n_b])
            copies.store(q_s, outs[6 + n_b])
        copies.drain()

    outs = [narrow] * 4 + [wide] + probs_shapes + tails
    scratch = (
        [narrow, ((rows, LANES), F32), ((16, width), BF16), ((4, width, width), BF16)]
        + [narrow] * 4
        + [wide, ((rows, width), BF16 if final else F32)]
        + probs_shapes
    )
    flat = [w for pair in weights for w in pair]
    return kernel_call(
        body,
        control,
        list(xs) + [flags] + list(vecs) + flat,
        outs,
        scratch,
        n_x + 6 + n_rest + n_b + 1 + n_t,
        8 * rows * width * width,
        8 * width * width + 20 * rows * width,
        name,
    )


def ffn_forward(control, middle, vecs, w_inner, w_outer, name):
    rows, width = middle.shape
    narrow, wide = ((rows, width), BF16), ((rows, width), F32)
    hidden = ((BLOCKS, rows, width), BF16)

    def body(first, ins, outs, scr, copies):
        middle_in, vec_a, vec_b, wi_a, wi_b, wo_a, wo_b = ins
        mid_s, vec_s, wi_s, wo_s, mb_s, inner_s, acc_s, act_s, slope_s, out_s = scr
        mid_load = copies.load(middle_in, mid_s)
        vec_load = copies.load_either(first, vec_a, vec_b, vec_s)
        wi_loads, wo_loads = [], []
        for j in range(BLOCKS):
            part = pl.ds(j * width, width)
            wi_loads.append(
                copies.load_either(first, wi_a.at[:, part], wi_b.at[:, part], wi_s.at[j])
            )
            wo_loads.append(
                copies.load_either(first, wo_a.at[part, :], wo_b.at[part, :], wo_s.at[j])
            )
        mid_load.wait()
        vec_load.wait()
        vec = vec_s[...].astype(F32)
        mb_s[...] = mid_s[...].astype(BF16)
        for j in range(BLOCKS):
            wi_loads[j].wait()
            inner_s[...] = mm(mb_s[...], wi_s[j])

            def activate(where):
                inner = inner_s[where, :] + vec[8 + j : 9 + j]
                phi = 0.5 * (1.0 + lax.erf(inner * (0.5**0.5)))
                act_s[where, :] = (inner * phi).astype(BF16)
                density = jnp.exp(-0.5 * inner * inner) * 0.3989422804014327
                slope_s[j, where, :] = (phi + inner * density).astype(BF16)

            each_rows(rows, 16, activate)
            copies.store(slope_s.at[j], outs[0].at[j])
            wo_loads[j].wait()
            product = mm(act_s[...], wo_s[j])
            acc_s[...] = product if j == 0 else acc_s[...] + product

        def finish(where):
            after = mid_s[where, :] + (acc_s[where, :] + vec[5:6])
            acc_s[where, :] = after
            normed, _ = norm_stats(after)
            out_s[where, :] = (normed * vec[6:7] + vec[7:8]).astype(BF16)

        each_rows(rows, 32, finish)
        copies.store(acc_s, outs[1])
        copies.store(out_s, outs[2])
        copies.drain()

    weights = ((BLOCKS, width, width), BF16)
    return kernel_call(
        body,
        control,
        [middle] + list(vecs) + list(w_inner) + list(w_outer),
        [hidden, wide, narrow],
        [wide, ((16, width), BF16), weights, weights, narrow, wide, wide, narrow, hidden, narrow],
        2 + 4 * BLOCKS + 2,
        16 * rows * width * width,
        16 * width * width + 26 * rows * width,
        name,
    )


def ffn_backward(control, grad_out, middle, saved, vecs, w_inner, w_outer, buffer, name):
    slope, after = saved
    rows, width = grad_out.shape
    narrow, wide = ((rows, width), BF16), ((rows, width), F32)
    hidden = ((BLOCKS, rows, width), BF16)

    def body(first, ins, outs, scr, copies):
        g_in, mid_in, slope_in, after_in, vec_a, vec_b, wi_a, wi_b, wo_a, wo_b = ins[:10]
        gmid_out, extra_out, pair_out = outs
        g_s, mid_s, slope_s, after_s, vec_s, wi_s, wo_s, go_s, gi_s, acc_s, sums_s, extra_s = scr
        g_load = copies.load(g_in, g_s)
        after_load = copies.load(after_in, after_s)
        vec_load = copies.load_either(first, vec_a, vec_b, vec_s)
        loads = []
        for j in range(BLOCKS):
            part = pl.ds(j * width, width)
            loads.append(
                (
                    copies.load_either(first, wo_a.at[part, :], wo_b.at[part, :], wo_s.at[j]),
                    copies.load(slope_in.at[j], slope_s.at[j]),
                    copies.load_either(first, wi_a.at[:, part], wi_b.at[:, part], wi_s.at[j]),
                )
            )
        mid_load = copies.load(mid_in, mid_s)
        g_load.wait()
        after_load.wait()
        vec_load.wait()
        vec = vec_s[...].astype(F32)
        sums_s[...] = jnp.zeros_like(sums_s)

        def start(where):
            grad = g_s[where, :].astype(F32)
            normed, inverse = norm_stats(after_s[where, :])
            sums_s[0] += folded(grad * normed)
            sums_s[1] += folded(grad)
            grad_after = norm_back(grad, normed, inverse, vec[6:7])
            acc_s[where, :] = grad_after
            rounded = grad_after.astype(BF16)
            go_s[where, :] = rounded
            sums_s[2] += folded(rounded.astype(F32))

        each_rows(rows, 32, start)
        copies.store(go_s, pair_out.at[pl.ds(rows, rows)])
        extra_s[...] = jnp.zeros_like(extra_s)
        for i in range(3):
            extra_s[i : i + 1, :] = jnp.sum(sums_s[i], 0, keepdims=True)
        copies.store(extra_s, extra_out)
        for j in range(BLOCKS):
            for load in loads[j]:
                load.wait()
            gi_s[...] = (mm_nt(go_s[...], wo_s[j]) * slope_s[j].astype(F32)).astype(BF16)
            acc_s[...] += mm_nt(gi_s[...], wi_s[j])
        copies.store(acc_s, gmid_out)
        mid_load.wait()
        copies.store(mid_s, pair_out.at[pl.ds(0, rows)])
        copies.drain()

    weights = ((BLOCKS, width, width), BF16)
    inputs = [grad_out, middle, slope, after] + list(vecs) + list(w_inner) + list(w_outer)
    aliases = {}
    if buffer is not None:
        inputs = inputs + [buffer]
        aliases = {len(inputs): 2}
    return kernel_call(
        body,
        control,
        inputs,
        [wide, ((8, width), F32), ((2 * rows, width), BF16)],
        [
            narrow,
            narrow,
            hidden,
            wide,
            ((16, width), BF16),
            weights,
            weights,
            narrow,
            narrow,
            wide,
            ((8, 8, width), F32),
            ((8, width), F32),
        ],
        3 + 3 * BLOCKS + 1 + 4,
        16 * rows * width * width,
        16 * width * width + 30 * rows * width,
        name,
        aliases,
    )


def ffn_weight_grads(control, pieces, vecs, w_inner, w_outer, name):
    rows, width = pieces[0].shape[0] // 2, pieces[0].shape[1]
    count = len(pieces)
    narrow, wide = ((rows, width), BF16), ((rows, width), F32)
    tall = ((count * rows, width), BF16)

    def body(first, block, ins, outs, scr, copies):
        piece_in = ins[:count]
        vec_a, vec_b, wi_a, wi_b, wo_a, wo_b = ins[count : count + 6]
        mid_s, go_s, gi_s, act_s, vec_s, wi_s, wo_s, inner_s, back_s, gw_s, sums_s, extra_s = scr
        part = pl.ds(pl.multiple_of(block * width, width), width)
        vec_load = copies.load_either(first, vec_a, vec_b, vec_s)
        wi_load = copies.load_either(first, wi_a.at[:, part], wi_b.at[:, part], wi_s)
        wo_load = copies.load_either(first, wo_a.at[part, :], wo_b.at[part, :], wo_s)
        loads = []
        for i, piece in enumerate(piece_in):
            spot = pl.ds(i * rows, rows)
            loads.append(
                (
                    copies.load(piece.at[pl.ds(0, rows)], mid_s.at[spot]),
                    copies.load(piece.at[pl.ds(rows, rows)], go_s.at[spot]),
                )
            )
        vec_load.wait()
        wi_load.wait()
        wo_load.wait()
        extra_s[...] = vec_s[...].astype(F32)
        bias = extra_s[pl.ds(8 + block, 1), :]
        sums_s[...] = jnp.zeros_like(sums_s)
        for i in range(count):
            for load in loads[i]:
                load.wait()
            spot = slice(i * rows, (i + 1) * rows)
            inner_s[...] = mm(mid_s[spot, :], wi_s[...])
            back_s[...] = mm_nt(go_s[spot, :], wo_s[...])

            def turn(where, base=i * rows):
                inner = inner_s[where, :] + bias
                phi = 0.5 * (1.0 + lax.erf(inner * (0.5**0.5)))
                density = jnp.exp(-0.5 * inner * inner) * 0.3989422804014327
                target = pl.ds(pl.multiple_of(base + where.start, 16), where.size)
                act_s[target, :] = (inner * phi).astype(BF16)
                rounded = (back_s[where, :] * (phi + inner * density)).astype(BF16)
                gi_s[target, :] = rounded
                sums_s[...] += folded(rounded.astype(F32))

            each_rows(rows, 16, turn)
        gw_s[pl.ds(0, width), :] = mm_tn(mid_s[...], gi_s[...]).astype(BF16)
        copies.store(gw_s.at[pl.ds(0, width)], outs[0].at[pl.ds(0, width)])
        gw_s[pl.ds(width, width), :] = mm_tn(act_s[...], go_s[...]).astype(BF16)
        tail = jnp.concatenate(
            [jnp.sum(sums_s[...], 0, keepdims=True), jnp.zeros((EXTRA - 1, width), F32)], 0
        )
        gw_s[pl.ds(2 * width, EXTRA), :] = tail.astype(BF16)
        copies.store(gw_s.at[pl.ds(width, width + EXTRA)], outs[0].at[pl.ds(width, width + EXTRA)])
        copies.drain()

    square = ((width, width), BF16)
    return kernel_call(
        body,
        control,
        list(pieces) + list(vecs) + list(w_inner) + list(w_outer),
        [((2 * width + EXTRA, width), BF16)],
        [
            tall,
            tall,
            tall,
            tall,
            ((16, width), BF16),
            square,
            square,
            wide,
            wide,
            ((2 * width + EXTRA, width), BF16),
            ((8, width), F32),
            ((16, width), F32),
        ],
        3 + 2 * count + 2,
        8 * count * rows * width * width,
        4 * width * width + 4 * count * rows * width,
        name,
        with_block=True,
    )[0]


def attn_backward(control, grads, saved, xs, flags, vecs, weights, extra, blocks, buffers, name):
    query, key, value, ctx, before = saved[:5]
    probs = saved[5 : 5 + len(blocks)]
    rows, width = query.shape
    narrow, wide = ((rows, width), BF16), ((rows, width), F32)
    probs_shapes = [((PAIRS, 2 * nq, nk), BF16) for _, nq, _, _, nk, _ in blocks]
    n_x, n_b, n_g = len(xs), len(blocks), len(grads)
    kind = grads[0].dtype
    total_rows = 4 * width + EXTRA

    def body(first, ins, outs, scr, copies):
        g_in, x_in = ins[:n_g], ins[n_g : n_g + n_x]
        q_in, k_in, v_in, ctx_in, before_in = ins[n_g + n_x : n_g + n_x + 5]
        rest = ins[n_g + n_x + 5 :]
        probs_in, flags_in, vec_in, w_in = rest[:n_b], rest[n_b], rest[n_b + 1 : n_b + 3], rest[
            n_b + 3 : n_b + 11
        ]
        extra_in = rest[n_b + 11]
        (
            g_s,
            x_s,
            q_s,
            k_s,
            v_s,
            ctx_s,
            before_s,
            flags_s,
            vec_s,
            w_s,
            gb_s,
            gctx_s,
            gq_s,
            gk_s,
            gv_s,
            gx_s,
            gw_s,
            sums_s,
            extra_s,
        ) = scr[:19]
        probs_s = scr[19:]

        def load_rows(pieces, target):
            at, loads = 0, []
            for piece in pieces:
                loads.append(copies.load(piece, target.at[pl.ds(at, piece.shape[0])]))
                at += piece.shape[0]
            return loads

        g_loads = load_rows(g_in, g_s)
        early = [copies.load(before_in, before_s)]
        vec_load = copies.load_either(first, vec_in[0], vec_in[1], vec_s)
        wo_load = copies.load_either(first, w_in[6], w_in[7], w_s.at[3])
        flags_load = copies.load(flags_in, flags_s)
        heads = [copies.load(a, b) for a, b in ((q_in, q_s), (k_in, k_s), (v_in, v_s))]
        probs_loads = [copies.load(a, b) for a, b in zip(probs_in, probs_s)]
        w_loads = [
            copies.load_either(first, w_in[2 * i], w_in[2 * i + 1], w_s.at[i]) for i in range(3)
        ]
        ctx_load = copies.load(ctx_in, ctx_s)
        x_loads = load_rows(x_in, x_s)
        extra_s[...] = jnp.zeros_like(extra_s)
        extra_load = copies.load(extra_in, extra_s.at[pl.ds(8, 8)])
        for load in g_loads + early + [vec_load]:
            load.wait()
        vec = vec_s[...].astype(F32)
        sums_s[...] = jnp.zeros_like(sums_s)

        def start(where):
            grad = g_s[where, :].astype(F32)
            normed, inverse = norm_stats(before_s[where, :])
            sums_s[3] += folded(grad * normed)
            sums_s[4] += folded(grad)
            grad_before = norm_back(grad, normed, inverse, vec[3:4])
            before_s[where, :] = grad_before
            rounded = grad_before.astype(BF16)
            gb_s[where, :] = rounded
            sums_s[2] += folded(rounded.astype(F32))

        each_rows(rows, 32, start)
        wo_load.wait()
        gctx_s[...] = mm_nt(gb_s[...], w_s[3]).astype(BF16)
        flags_load.wait()
        for load in heads:
            load.wait()
        for index, (q0, nq, iq, k0, nk, ik) in enumerate(blocks):
            probs_loads[index].wait()
            low, high, is_low = half_masks(nq)

            def pair_turn(pair, carry):
                lanes = pl.ds(pl.multiple_of(pair * LANES, LANES), LANES)
                keep = head_keep(pair, flags_s[pl.ds(q0, nq), :]).astype(BF16)
                g2 = stacked_halves(gctx_s[pl.ds(q0, nq), lanes] * keep, low, high)
                q2 = stacked_halves(q_s[pl.ds(q0, nq), lanes], low, high)
                k_piece = k_s[pl.ds(k0, nk), lanes]
                kept = probs_s[index][pair]
                wide_probs = kept.astype(F32)
                g_probs = mm_nt(g2, v_s[pl.ds(k0, nk), lanes])
                inner = jnp.sum(wide_probs * g_probs, -1, keepdims=True)
                g_scores = (wide_probs * (g_probs - inner)).astype(BF16)
                scale = HEAD_DIM ** (-0.5)
                g_q = mm(g_scores, k_piece) * scale
                gq_s[pl.ds(q0, nq), lanes] = jnp.where(is_low, g_q[:nq], g_q[nq:]).astype(BF16)
                gk_s[pl.ds(k0, nk), lanes] = (mm_tn(g_scores, q2) * scale).astype(BF16)
                gv_s[pl.ds(k0, nk), lanes] = mm_tn(kept, g2).astype(BF16)
                return carry

            lax.fori_loop(0, PAIRS, pair_turn, 0, unroll=2)
        for load in w_loads:
            load.wait()
        grad_x = before_s[...] + mm_nt(gq_s[...], w_s[0])
        grad_x = grad_x + mm_nt(gk_s[...], w_s[1])
        grad_x = grad_x + mm_nt(gv_s[...], w_s[2])
        gx_s[...] = grad_x.astype(BF16)
        at = 0
        for target in outs[:n_x]:
            copies.store(gx_s.at[pl.ds(at, target.shape[0])], target)
            at += target.shape[0]
        keep_out, send_out = outs[n_x], outs[n_x + 1]
        for load in x_loads + [ctx_load]:
            load.wait()
        for i, (left, right) in enumerate(
            ((x_s, gq_s), (x_s, gk_s), (x_s, gv_s), (ctx_s, gb_s))
        ):
            spot = pl.ds(i * width, width)
            gw_s[spot, :] = mm_tn(left[...], right[...]).astype(BF16)
            copies.store_either(first, gw_s.at[spot], keep_out.at[spot], send_out.at[spot])

        def bias_sums(where):
            sums_s[0] += folded(gq_s[where, :].astype(F32))
            sums_s[1] += folded(gv_s[where, :].astype(F32))

        each_rows(rows, 32, bias_sums)
        extra_load.wait()
        for i in range(5):
            extra_s[i : i + 1, :] = jnp.sum(sums_s[i], 0, keepdims=True)
        spot = pl.ds(4 * width, EXTRA)
        gw_s[spot, :] = extra_s[...].astype(BF16)
        copies.store_either(first, gw_s.at[spot], keep_out.at[spot], send_out.at[spot])
        copies.drain()

    flat = [w for pair in weights for w in pair]
    inputs = (
        list(grads)
        + list(xs)
        + [query, key, value, ctx, before]
        + list(probs)
        + [flags]
        + list(vecs)
        + flat
        + [extra]
    )
    aliases = {}
    if buffers is not None:
        aliases = {len(inputs) + 1: n_x, len(inputs) + 2: n_x + 1}
        inputs = inputs + list(buffers)
    return kernel_call(
        body,
        control,
        inputs,
        [((x.shape[0], width), BF16) for x in xs] + [((total_rows, width), BF16)] * 2,
        [((rows, width), kind)]
        + [narrow] * 5
        + [wide, ((rows, LANES), F32), ((16, width), BF16), ((4, width, width), BF16)]
        + [narrow] * 6
        + [((total_rows, width), BF16), ((8, 8, width), F32), ((EXTRA, width), F32)]
        + probs_shapes,
        n_g + 2 * n_x + 1 + 1 + 4 + 1 + 3 + n_b + 1 + 4 + 1 + 1,
        16 * rows * width * width,
        16 * width * width + 30 * rows * width,
        name,
        aliases,
    )


def swapper(sections):
    n = lax.axis_size("dp")

    def swap(value, bit):
        pairs = [(s * n + i, s * n + (i ^ bit)) for s in sections for i in range(n)]
        return lax.ppermute(value, ("section", "dp"), pairs)

    return swap


def spread_sum(part, bits, swap):
    at = lax.axis_index("dp")
    for bit in bits:
        side = (at // bit) % 2
        half = part.shape[0] // 2
        keep = lax.dynamic_slice_in_dim(part, side * half, half, 0)
        send = lax.dynamic_slice_in_dim(part, (1 - side) * half, half, 0)
        part = keep + swap(send, bit)
    return part


def gather_back(part, bits, swap):
    at = lax.axis_index("dp")
    for bit in reversed(bits):
        side = (at // bit) % 2
        far = swap(part, bit)
        part = jnp.where(side == 0, jnp.concatenate([part, far]), jnp.concatenate([far, part]))
    return part


def per_device(
    tokens,
    cotangent,
    task_flags,
    w_query,
    w_key,
    w_value,
    w_attn_out,
    b_query,
    b_value,
    b_attn_out,
    norm1_gain,
    norm1_bias,
    w_inner,
    b_inner,
    w_outer,
    b_outer,
    norm2_gain,
    norm2_bias,
):
    section = lax.axis_index("section")
    stage, core = section // 2, section % 2
    items, seq_len, width = tokens.shape
    words = seq_len - OBJ
    n_visual, n_word = items * OBJ, items * words
    is_first = stage == 0

    def swap_stage(value):
        return lax.ppermute(value, "section", [(0, 2), (1, 3), (2, 0), (3, 1)])

    def swap_core(value):
        return lax.ppermute(value, "section", [(0, 1), (1, 0), (2, 3), (3, 2)])

    flags_far = swap_stage(task_flags)
    tokens_far = swap_stage(tokens)
    attn_w = [w[0] for w in (w_query, w_key, w_value, w_attn_out)]
    vec = jnp.concatenate(
        [
            b_query,
            b_value,
            b_attn_out,
            norm1_gain,
            norm1_bias,
            b_outer,
            norm2_gain,
            norm2_bias,
            b_inner.reshape(BLOCKS, width),
            jnp.zeros((4, width), BF16),
        ],
        0,
    )
    vecs = (vec, swap_core(vec))
    attn_w = [(w, swap_core(w)) for w in attn_w]
    inner_w = (w_inner[0], swap_core(w_inner[0]))
    outer_w = (w_outer[0], swap_core(w_outer[0]))
    cot_far = swap_stage(cotangent)

    flags = task_flags.astype(F32)
    far = flags_far.astype(F32)
    flags = jnp.where(
        is_first, jnp.concatenate([flags, far]), jnp.concatenate([far, flags])
    )
    flags_v = jnp.broadcast_to(jnp.repeat(flags, OBJ)[:, None], (2 * n_visual, LANES))
    flags_w = jnp.broadcast_to(jnp.repeat(flags, words)[:, None], (2 * n_word, LANES))
    flags_all = jnp.concatenate([flags_v, flags_w], 0)

    def split(first, second):
        visual = jnp.concatenate([first[:, :OBJ], second[:, :OBJ]], 0)
        word = jnp.concatenate([first[:, OBJ:], second[:, OBJ:]], 0)
        return visual.reshape(2 * n_visual, width), word.reshape(2 * n_word, width)

    place = lax.axis_index("dp")
    side = place % 2
    block = 2 * side + core

    def control(at, parity):
        return jnp.stack([stage == at, core == parity, block]).astype(jnp.int32)

    even_0, odd_0, even_1, odd_1 = control(0, 0), control(0, 1), control(1, 0), control(1, 1)
    even_any = jnp.stack([core >= 0, core == 0, block]).astype(jnp.int32)
    blocks_v = [(g * n_visual, n_visual, OBJ, g * n_visual, n_visual, OBJ) for g in (0, 1)]
    blocks_w = [(g * n_word, n_word, words, g * n_word, n_word, words) for g in (0, 1)]
    blocks_x = []
    for g in (0, 1):
        v_at, w_at = g * n_visual, 2 * n_visual + g * n_word
        blocks_x.append((v_at, n_visual, OBJ, w_at, n_word, words))
        blocks_x.append((w_at, n_word, words, v_at, n_visual, OBJ))

    visual_0, word_0 = split(tokens, tokens_far)
    grad_v4, grad_w4 = split(cot_far, cotangent)
    ffn_w = (vecs, inner_w, outer_w)

    *kept_0, middle_0, mid_0 = attn_forward(
        even_0, [visual_0], flags_v, vecs, attn_w, blocks_v, False, "s0_attn_f"
    )
    *ffn_0, visual_1 = ffn_forward(even_0, middle_0, *ffn_w, "s0_ffn_f")
    *kept_1, visual_2, word_2 = attn_forward(
        odd_0, [visual_1, word_0], flags_all, vecs, attn_w, blocks_x, True, "s1_attn_f"
    )
    word_2, visual_2 = swap_stage(word_2), swap_stage(visual_2)
    *kept_3, middle_3, mid_3 = attn_forward(
        odd_1, [word_2], flags_w, vecs, attn_w, blocks_w, False, "s3_attn_f"
    )
    *ffn_3, word_4 = ffn_forward(odd_1, middle_3, *ffn_w, "s3_ffn_f")
    gmid_3, extra_3, pair_3 = ffn_backward(odd_1, grad_w4, mid_3, ffn_3, *ffn_w, None, "s3_ffn_b")
    grad_w2, *sums = attn_backward(
        odd_1,
        [gmid_3],
        kept_3,
        [word_2],
        flags_w,
        vecs,
        attn_w,
        extra_3,
        blocks_w,
        None,
        "s3_attn_b",
    )
    *kept_2, middle_2, mid_2 = attn_forward(
        even_1, [visual_2], flags_v, vecs, attn_w, blocks_v, False, "s2_attn_f"
    )
    *ffn_2, visual_4 = ffn_forward(even_1, middle_2, *ffn_w, "s2_ffn_f")
    gmid_2, extra_2, pair_2 = ffn_backward(even_1, grad_v4, mid_2, ffn_2, *ffn_w, None, "s2_ffn_b")
    grad_v2, *sums = attn_backward(
        even_1,
        [gmid_2],
        kept_2,
        [visual_2],
        flags_v,
        vecs,
        attn_w,
        extra_2,
        blocks_v,
        sums,
        "s2_attn_b",
    )

    def join(visual, word):
        return jnp.concatenate(
            [visual.reshape(items, OBJ, width), word.reshape(items, words, width)], 1
        )

    grad_w2, grad_v2 = swap_stage(grad_w2), swap_stage(grad_v2)
    mixed_far = swap_stage(join(visual_4[:n_visual], word_4[:n_word]))
    mixed = jnp.where(is_first, mixed_far, join(visual_4[n_visual:], word_4[n_word:]))
    grad_v1, grad_w0, *sums = attn_backward(
        odd_0,
        [grad_v2, grad_w2],
        kept_1,
        [visual_1, word_0],
        flags_all,
        vecs,
        attn_w,
        jnp.zeros((8, width), F32),
        blocks_x,
        sums,
        "s1_attn_b",
    )
    gmid_0, extra_0, pair_0 = ffn_backward(
        even_0, grad_v1, mid_0, ffn_0, *ffn_w, pair_2, "s0_ffn_b"
    )
    grad_v0, keep, send = attn_backward(
        even_0,
        [gmid_0],
        kept_0,
        [visual_0],
        flags_v,
        vecs,
        attn_w,
        extra_0,
        blocks_v,
        sums,
        "s0_attn_b",
    )

    swap_all, swap_late = swapper(range(4)), swapper((2, 3))
    line = []
    while 2 ** (len(line) + 1) < lax.axis_size("dp"):
        line.append(2 ** (len(line) + 1))

    def ffn_sums(pair, control, swap, name):
        across = swap(pair, 1)
        pieces = [pair, across, swap_core(pair), swap_core(across)]
        sums = ffn_weight_grads(control, pieces, *ffn_w, name)
        parts = []
        for piece in (sums[:width], sums[width:]):
            piece = gather_back(spread_sum(piece, line, swap), [1] + line, swap)
            parts.append((piece, swap_core(piece)))
        return parts

    ffn_odd = ffn_sums(pair_3, odd_1, swap_late, "s3_ffn_w")
    ffn_even = ffn_sums(pair_0, even_any, swap_all, "even_ffn_w")
    attn = []
    for piece in (slice(0, 2 * width), slice(2 * width, None)):
        part = keep[piece] + swap_core(send[piece])
        attn.append(
            gather_back(spread_sum(part, [1] + line, swap_all), [1] + line, swap_all).astype(F32)
        )

    grad_v0, grad_w0, _ = lax.optimization_barrier((grad_v0, grad_w0, attn[1]))
    grad_far = swap_stage(join(grad_v0[n_visual:], grad_w0[n_word:]))
    tokens_grad = jnp.where(is_first, join(grad_v0[:n_visual], grad_w0[:n_word]), grad_far)

    is_even = core == 0
    unused = section == 1

    def pick(even, odd):
        return jnp.where(is_even, even, jnp.where(unused, jnp.zeros_like(odd), odd)).astype(F32)

    by_core = []
    for c in (0, 1):
        by_core.append([pick(ffn_even[h][c], ffn_odd[h][1 - c]) for h in (0, 1)])
    size = width + EXTRA
    inner, outer, inner_bias = [], [], []
    for x in (0, 1):
        for c in (0, 1):
            inner.append(by_core[c][0][x * width : (x + 1) * width])
            outer.append(by_core[c][1][x * size : x * size + width])
            inner_bias.append(by_core[c][1][x * size + width : x * size + width + 1])
    square = [attn[i // 2][(i % 2) * width : (i % 2 + 1) * width] for i in range(4)]
    small = attn[1][2 * width :]
    small = small * jnp.where(unused & (jnp.arange(EXTRA)[:, None] >= 8), 0.0, 1.0)
    return (
        mixed,
        tokens_grad,
        square[0][None],
        square[1][None],
        square[2][None],
        square[3][None],
        small[0:1],
        small[1:2],
        small[2:3],
        small[3:4],
        small[4:5],
        jnp.concatenate(inner, 1)[None],
        jnp.concatenate(inner_bias, 1),
        jnp.concatenate(outer, 0)[None],
        small[10:11],
        small[8:9],
        small[9:10],
    )


def solution(mesh):
    tokens = P(("section", "dp"), None, None)
    matrix = P("section", None, None)
    vector = P("section", None)
    placed = (
        (tokens, tokens, P(("section", "dp")))
        + (matrix,) * 4
        + (vector,) * 5
        + (matrix, vector, matrix)
        + (vector,) * 3
    )
    return jax.shard_map(
        per_device,
        mesh=mesh,
        in_specs=placed,
        out_specs=(tokens, tokens)
        + (matrix,) * 4
        + (vector,) * 5
        + (matrix, vector, matrix)
        + (vector,) * 3,
        check_vma=False,
    )
```

```python
import jax
import jax.numpy as jnp
from jax import lax
from jax.experimental import pallas as pl
from jax.experimental.pallas import tpu as pltpu
from jax.sharding import PartitionSpec as P

HEADS = 12
HEAD_DIM = 64
OBJ = 36
PAIRS = HEADS // 2
EPS = 1e-06
NEG = -1000000000.0
F32 = jnp.float32
BF16 = jnp.bfloat16
LANES = 128
BLOCKS = 4
EXTRA = 32
GROUP = 8
VMEM = 60 * 1024 * 1024
FLOPS_PER_US = 1.15e9
PLAN = ("m2", "ce", "co", "ce", "m3", "B01", "co", "ce", "ce", "co", "B23", "co", "end", "ce")


def mm(a, b):
    return jnp.dot(a, b, preferred_element_type=F32)


def mm_nt(a, b):
    return lax.dot_general(a, b, (((1,), (1,)), ((), ())), preferred_element_type=F32)


def mm_tn(a, b):
    return lax.dot_general(a, b, (((0,), (0,)), ((), ())), preferred_element_type=F32)


def each_rows(count, step, body):
    def turn(i, carry):
        body(pl.ds(pl.multiple_of(i * step, step), step))
        return carry

    lax.fori_loop(0, count // step, turn, 0)


def folded(values):
    rows, width = values.shape
    return jnp.sum(values.reshape(rows // 8, 8, width), 0)


class Copies:
    def __init__(self, sems):
        self.sems, self.used, self.stores = sems, 0, []

    def next_sem(self):
        self.used += 1
        return self.sems.at[self.used - 1]

    def load(self, source, target):
        copy = pltpu.make_async_copy(source, target, self.next_sem())
        copy.start()
        return copy

    def load_either(self, first, own, other, target):
        sem = self.next_sem()
        mine = pltpu.make_async_copy(own, target, sem)

        @pl.when(first)
        def _():
            mine.start()

        @pl.when(jnp.logical_not(first))
        def _():
            pltpu.make_async_copy(other, target, sem).start()

        return mine

    def store(self, source, target, alone=False):
        copy = pltpu.make_async_copy(source, target, self.next_sem())
        copy.start()
        if not alone:
            self.stores.append(copy)
        return copy

    def store_either(self, first, source, target, other):
        sem = self.next_sem()
        mine = pltpu.make_async_copy(source, target, sem)

        @pl.when(first)
        def _():
            mine.start()

        @pl.when(jnp.logical_not(first))
        def _():
            pltpu.make_async_copy(source, other, sem).start()

        self.stores.append(mine)

    def drain(self):
        for copy in self.stores:
            copy.wait()
        self.stores = []


class Control:
    def __init__(self, scalars, order):
        self.scalars, self.order = jnp.stack(scalars).astype(jnp.int32), order


def kernel_call(body, control, inputs, outs, scratch, sems, micros, name, aliases=None, more=0):
    n_in, n_out = len(inputs), len(outs)
    after = control.order
    inputs = list(inputs) + list(after)
    outs = list(outs) + [((8, LANES), F32)]

    def kernel(control_ref, *refs):
        @pl.when(control_ref[0] == 1)
        def _():
            body(
                control_ref[1] == 1,
                control_ref[2],
                refs[:n_in],
                refs[len(inputs) : len(inputs) + n_out],
                refs[len(inputs) + n_out + 1 : -1],
                Copies(refs[-1]),
                *[control_ref[3 + i] for i in range(more)],
            )

    *results, token = pl.pallas_call(
        kernel,
        out_shape=[jax.ShapeDtypeStruct(shape, kind) for shape, kind in outs],
        in_specs=[pl.BlockSpec(memory_space=pltpu.SMEM)]
        + [pl.BlockSpec(memory_space=pl.ANY)] * len(inputs),
        out_specs=[pl.BlockSpec(memory_space=pl.ANY)] * len(outs),
        scratch_shapes=[pltpu.VMEM(shape, kind) for shape, kind in scratch]
        + [pltpu.SemaphoreType.DMA((sems,))],
        input_output_aliases=aliases or {},
        compiler_params=pltpu.CompilerParams(vmem_limit_bytes=VMEM),
        cost_estimate=pl.CostEstimate(
            flops=int(micros * FLOPS_PER_US), bytes_accessed=0, transcendentals=0
        ),
        name=name,
    )(control.scalars, *inputs)
    after[:] = [token]
    return results


def norm_stats(values):
    centered = values - jnp.mean(values, -1, keepdims=True)
    inverse = lax.rsqrt(jnp.mean(centered * centered, -1, keepdims=True) + EPS)
    return centered * inverse, inverse


def norm_back(grad_out, normed, inverse, gain):
    scaled = grad_out * gain
    return inverse * (
        scaled
        - jnp.mean(scaled, -1, keepdims=True)
        - normed * jnp.mean(scaled * normed, -1, keepdims=True)
    )


def head_keep(pair, flags):
    lane = lax.broadcasted_iota(jnp.int32, flags.shape, 1)
    head = 2 * pair + jnp.where(lane >= HEAD_DIM, 1, 0)
    return jnp.where(lax.rem(head, 3).astype(F32) != flags, 1.0, 0.0)


def half_masks(rows):
    lane = lax.broadcasted_iota(jnp.int32, (rows, LANES), 1)
    low = jnp.where(lane < HEAD_DIM, 1.0, 0.0)
    return low.astype(BF16), (1.0 - low).astype(BF16), lane < HEAD_DIM


def stacked_halves(piece, low, high):
    return jnp.concatenate([piece * low, piece * high], 0)


def project(x_s, vec, w_s, loads, q_s, k_s, v_s):
    for i, (target, bias) in enumerate(((q_s, 0), (k_s, None), (v_s, 1))):
        loads[i].wait()
        product = mm(x_s[...], w_s[i])
        if bias is not None:
            product = product + vec[bias : bias + 1]
        target[...] = product.astype(BF16)


def attend(blocks, flags_s, flags_at, q_s, k_s, v_s, ctx_s, probs_s):
    for index, (q0, nq, iq, k0, nk, ik) in enumerate(blocks):
        low, high, is_low = half_masks(nq)
        row = lax.broadcasted_iota(jnp.int32, (nq, nk), 0) // iq
        col = lax.broadcasted_iota(jnp.int32, (nq, nk), 1) // ik
        apart = jnp.where(row == col, 0.0, 1.0)
        apart = jnp.concatenate([apart, apart], 0) > 0.0

        def pair_turn(pair, carry):
            lanes = pl.ds(pl.multiple_of(pair * LANES, LANES), LANES)
            q2 = stacked_halves(q_s[pl.ds(q0, nq), lanes], low, high)
            scores = mm_nt(q2, k_s[pl.ds(k0, nk), lanes]) * (HEAD_DIM ** (-0.5))
            scores = jnp.where(apart, NEG, scores)
            shifted = jnp.exp(scores - jnp.max(scores, -1, keepdims=True))
            probs = (shifted / jnp.sum(shifted, -1, keepdims=True)).astype(BF16)
            probs_s[index][pair] = probs
            mixed = mm(probs, v_s[pl.ds(k0, nk), lanes])
            keep = head_keep(pair, flags_s[pl.ds(flags_at + q0, nq), :])
            ctx = jnp.where(is_low, mixed[:nq], mixed[nq:]) * keep
            ctx_s[pl.ds(q0, nq), lanes] = ctx.astype(BF16)
            return carry

        lax.fori_loop(0, PAIRS, pair_turn, 0, unroll=PAIRS)


def attn_finish(x_s, vec, before_s, targets):
    def finish(where):
        before = x_s[where, :].astype(F32) + (before_s[where, :] + vec[2:3])
        before_s[where, :] = before
        normed, _ = norm_stats(before)
        middle = normed * vec[3:4] + vec[4:5]
        for target in targets:
            target[where, :] = middle.astype(target.dtype)

    each_rows(x_s.shape[0], 32, finish)


def ffn_hidden(mid_s, vec, wi_s, wo_s, loads, inner_s, act_s, slope_s, acc_s):
    for j in range(BLOCKS):
        loads[2 * j].wait()
        inner_s[...] = mm(mid_s[...], wi_s[j])

        def activate(where):
            inner = inner_s[where, :] + vec[8 + j : 9 + j]
            phi = 0.5 * (1.0 + lax.erf(inner * (0.5**0.5)))
            act_s[where, :] = (inner * phi).astype(BF16)
            density = jnp.exp(-0.5 * inner * inner) * 0.3989422804014327
            slope_s[j, where, :] = (phi + inner * density).astype(BF16)

        each_rows(mid_s.shape[0], 32, activate)
        loads[2 * j + 1].wait()
        product = mm(act_s[...], wo_s[j])
        acc_s[...] = product if j == 0 else acc_s[...] + product


def ffn_finish(wide_s, acc_s, vec, out_s, at):
    def finish(where):
        after = wide_s[where, :] + (acc_s[where, :] + vec[5:6])
        acc_s[where, :] = after
        normed, _ = norm_stats(after)
        out_s[where, :] = (normed * vec[6:7] + vec[7:8]).astype(BF16)

    each_rows(wide_s.shape[0], 32, finish)


def ffn_back_start(g_s, after_s, vec, acc_s, go_s, sums_s):
    def start(where):
        grad = g_s[where, :].astype(F32)
        normed, inverse = norm_stats(after_s[where, :])
        sums_s[8] += folded(grad * normed)
        sums_s[9] += folded(grad)
        grad_after = norm_back(grad, normed, inverse, vec[6:7])
        acc_s[where, :] = grad_after
        rounded = grad_after.astype(BF16)
        go_s[where, :] = rounded
        sums_s[10] += folded(rounded.astype(F32))

    each_rows(g_s.shape[0], 32, start)


def ffn_back(go_s, slope_s, wi_s, wo_s, loads, gi_s, acc_s):
    for j in range(BLOCKS):
        for load in loads[j]:
            load.wait()
        gi_s[...] = (mm_nt(go_s[...], wo_s[j]) * slope_s[j].astype(F32)).astype(BF16)
        acc_s[...] += mm_nt(gi_s[...], wi_s[j])


def sum_rows(sums_s, extra_s, count):
    extra_s[...] = jnp.zeros_like(extra_s)
    for i in range(count):
        extra_s[i : i + 1, :] = jnp.sum(sums_s[i], 0, keepdims=True)


def load_attn_weights(copies, first, w_in, w_s):
    return [copies.load_either(first, w_in[2 * i], w_in[2 * i + 1], w_s.at[i]) for i in range(4)]


def load_ffn_weights(copies, first, w_in, wi_s, wo_s):
    wi_a, wi_b, wo_a, wo_b = w_in
    width = wi_s.shape[1]
    loads = []
    for j in range(BLOCKS):
        part = pl.ds(j * width, width)
        loads.append(copies.load_either(first, wi_a.at[:, part], wi_b.at[:, part], wi_s.at[j]))
        loads.append(copies.load_either(first, wo_a.at[part, :], wo_b.at[part, :], wo_s.at[j]))
    return loads


def probs_of(blocks):
    return [((PAIRS, 2 * nq, nk), BF16) for _, nq, _, _, nk, _ in blocks]


def first_stage_forward(control, visual, word, flags, weights, blocks_0, blocks_1, name):
    vecs, attn_w, inner_w, outer_w = weights
    rows, width = visual.shape
    total = rows + word.shape[0]
    narrow, wide = ((rows, width), BF16), ((rows, width), F32)
    tall, tall_wide = ((total, width), BF16), ((total, width), F32)
    hidden = ((BLOCKS, rows, width), BF16)
    square = ((4, width, width), BF16)
    flat = [w for pair in attn_w for w in pair]
    probs_0, probs_1 = probs_of(blocks_0), probs_of(blocks_1)

    def body(first, block, ins, outs, scr, copies):
        visual_in, word_in, flags_in, vec_a, vec_b = ins[:5]
        attn_in, ffn_in = ins[5:13], ins[13:17]
        x_s, flags_s, vec0_s, vec1_s, w0_s, w1_s, wi_s, wo_s = scr[:8]
        q_s, k_s, v_s, ctx_s, before_s, wide_s, mid_s, inner_s, acc_s, act_s, slope_s = scr[8:19]
        x1_s, q1_s, k1_s, v1_s, ctx1_s, before1_s, out_s = scr[19:26]
        p0_s, p1_s = scr[26 : 26 + len(probs_0)], scr[26 + len(probs_0) :]
        other = jnp.logical_not(first)
        x_load = copies.load(visual_in, x_s)
        vec0_load = copies.load_either(first, vec_a, vec_b, vec0_s)
        w0_loads = load_attn_weights(copies, first, attn_in, w0_s)
        flags_load = copies.load(flags_in, flags_s)
        ffn_loads = load_ffn_weights(copies, first, ffn_in, wi_s, wo_s)
        word_load = copies.load(word_in, x1_s.at[pl.ds(rows, total - rows)])
        vec1_load = copies.load_either(other, vec_a, vec_b, vec1_s)
        w1_loads = load_attn_weights(copies, other, attn_in, w1_s)
        x_load.wait()
        vec0_load.wait()
        vec = vec0_s[...].astype(F32)
        project(x_s, vec, w0_s, w0_loads, q_s, k_s, v_s)
        flags_load.wait()
        attend(blocks_0, flags_s, 0, q_s, k_s, v_s, ctx_s, p0_s)
        for i, source in enumerate((q_s, k_s, v_s, ctx_s)):
            copies.store(source, outs[i])
        for i, source in enumerate(p0_s):
            copies.store(source, outs[5 + i])
        w0_loads[3].wait()
        before_s[...] = mm(ctx_s[...], w0_s[3])
        attn_finish(x_s, vec, before_s, (wide_s, mid_s))
        copies.store(before_s, outs[4])
        at = 5 + len(p0_s)
        copies.store(mid_s, outs[at])
        ffn_hidden(mid_s, vec, wi_s, wo_s, ffn_loads, inner_s, act_s, slope_s, acc_s)
        copies.store(slope_s, outs[at + 1])
        ffn_finish(wide_s, acc_s, vec, x1_s, 0)
        copies.store(acc_s, outs[at + 2])
        copies.store(x1_s.at[pl.ds(0, rows)], outs[at + 3])
        at += 4
        word_load.wait()
        vec1_load.wait()
        vec = vec1_s[...].astype(F32)
        project(x1_s, vec, w1_s, w1_loads, q1_s, k1_s, v1_s)
        attend(blocks_1, flags_s, 0, q1_s, k1_s, v1_s, ctx1_s, p1_s)
        for i, source in enumerate((q1_s, k1_s, v1_s, ctx1_s)):
            copies.store(source, outs[at + i])
        for i, source in enumerate(p1_s):
            copies.store(source, outs[at + 5 + i])
        w1_loads[3].wait()
        before1_s[...] = mm(ctx1_s[...], w1_s[3])
        attn_finish(x1_s, vec, before1_s, (out_s,))
        copies.store(before1_s, outs[at + 4])
        at += 5 + len(p1_s)
        copies.store(out_s.at[pl.ds(0, rows)], outs[at])
        copies.store(out_s.at[pl.ds(rows, total - rows)], outs[at + 1])
        copies.drain()

    outs = [narrow] * 4 + [wide] + probs_0 + [narrow, hidden, wide, narrow]
    outs += [tall] * 4 + [tall_wide] + probs_1 + [narrow, ((total - rows, width), BF16)]
    scratch = [narrow, ((total, LANES), F32)] + [((16, width), BF16)] * 2
    scratch += [square, square, square, square]
    scratch += [narrow] * 4 + [wide, wide, narrow, wide, wide, narrow, hidden]
    scratch += [tall] * 5 + [tall_wide, tall] + probs_0 + probs_1
    results = kernel_call(
        body,
        control,
        [visual, word, flags] + list(vecs) + flat + list(inner_w) + list(outer_w),
        outs,
        scratch,
        len(outs) + 5 + 8 + 2 * BLOCKS,
        4 + rows / 20 + total / 50,
        name,
    )
    n_0, n_1 = 5 + len(probs_0), 5 + len(probs_1)
    kept_0, rest = results[:n_0], results[n_0:]
    mid_0, slope_0, after_0, visual_1 = rest[:4]
    kept_1, out = rest[4 : 4 + n_1], rest[4 + n_1 :]
    return kept_0, mid_0, (slope_0, after_0), visual_1, kept_1, out[0], out[1]


SECTION = (
    ("x", "g", "vec", "w", "wi", "wo", "q", "k", "v", "ctx", "before", "wide", "mid", "inner", "acc")
    + ("act", "slope", "out", "go", "gb", "gctx", "gq", "gk", "gv", "sums", "extra")
)


class Refs:
    def __init__(self, names, refs):
        for name, ref in zip(names, refs):
            setattr(self, name, ref)
        self.probs = refs[len(names) :]


def section_scratch(rows, width, blocks):
    narrow, wide = ((rows, width), BF16), ((rows, width), F32)
    hidden, square = ((BLOCKS, rows, width), BF16), ((4, width, width), BF16)
    kinds = {
        "vec": ((16, width), BF16),
        "slope": hidden,
        "sums": ((16, 8, width), F32),
        "extra": ((16, width), F32),
    }
    kinds.update({name: wide for name in ("before", "wide", "inner", "acc")})
    kinds.update({name: square for name in ("w", "wi", "wo")})
    return [kinds.get(name, narrow) for name in SECTION] + probs_of(blocks)


def attn_back_start(g_s, before_s, vec, gb_s, sums_s):
    def start(where):
        grad = g_s[where, :].astype(F32)
        normed, inverse = norm_stats(before_s[where, :])
        sums_s[3] += folded(grad * normed)
        sums_s[4] += folded(grad)
        grad_before = norm_back(grad, normed, inverse, vec[3:4])
        before_s[where, :] = grad_before
        rounded = grad_before.astype(BF16)
        gb_s[where, :] = rounded
        sums_s[2] += folded(rounded.astype(F32))

    each_rows(g_s.shape[0], 32, start)


def attend_back(blocks, flags_s, flags_at, gctx_s, q_s, k_s, v_s, probs_s, gq_s, gk_s, gv_s):
    for index, (q0, nq, iq, k0, nk, ik) in enumerate(blocks):
        low, high, is_low = half_masks(nq)

        def pair_turn(pair, carry):
            lanes = pl.ds(pl.multiple_of(pair * LANES, LANES), LANES)
            keep = head_keep(pair, flags_s[pl.ds(flags_at + q0, nq), :]).astype(BF16)
            g2 = stacked_halves(gctx_s[pl.ds(q0, nq), lanes] * keep, low, high)
            q2 = stacked_halves(q_s[pl.ds(q0, nq), lanes], low, high)
            k_piece = k_s[pl.ds(k0, nk), lanes]
            kept = probs_s[index][pair]
            wide_probs = kept.astype(F32)
            g_probs = mm_nt(g2, v_s[pl.ds(k0, nk), lanes])
            inner = jnp.sum(wide_probs * g_probs, -1, keepdims=True)
            g_scores = (wide_probs * (g_probs - inner)).astype(BF16)
            scale = HEAD_DIM ** (-0.5)
            g_q = mm(g_scores, k_piece) * scale
            gq_s[pl.ds(q0, nq), lanes] = jnp.where(is_low, g_q[:nq], g_q[nq:]).astype(BF16)
            gk_s[pl.ds(k0, nk), lanes] = (mm_tn(g_scores, q2) * scale).astype(BF16)
            gv_s[pl.ds(k0, nk), lanes] = mm_tn(kept, g2).astype(BF16)
            return carry

        lax.fori_loop(0, PAIRS, pair_turn, 0, unroll=PAIRS)


def input_grad(before_s, gq_s, gk_s, gv_s, w_s):
    grad_x = before_s[...] + mm_nt(gq_s[...], w_s[0])
    grad_x = grad_x + mm_nt(gk_s[...], w_s[1])
    return (grad_x + mm_nt(gv_s[...], w_s[2])).astype(BF16)


def section_round(first, r, x_in, g_in, weights_in, flags_s, flags_at, flags_load, blocks, copies, outs):
    vec_in, attn_in, ffn_in = weights_in
    out_out, mid_out, go_out, grad_out, kept_out, extra_out = outs
    x_load = copies.load(x_in, r.x)
    vec_load = copies.load_either(first, vec_in[0], vec_in[1], r.vec)
    w_loads = load_attn_weights(copies, first, attn_in, r.w)
    ffn_loads = load_ffn_weights(copies, first, ffn_in, r.wi, r.wo)
    g_load = copies.load(g_in, r.g)

    def run():
        x_load.wait()
        vec_load.wait()
        vec = r.vec[...].astype(F32)
        project(r.x, vec, r.w, w_loads, r.q, r.k, r.v)
        if flags_load:
            flags_load.pop().wait()
        attend(blocks, flags_s, flags_at, r.q, r.k, r.v, r.ctx, r.probs)
        copies.store(r.ctx, kept_out.at[0])
        w_loads[3].wait()
        r.before[...] = mm(r.ctx[...], r.w[3])
        attn_finish(r.x, vec, r.before, (r.wide, r.mid))
        copies.store(r.mid, mid_out)
        ffn_hidden(r.mid, vec, r.wi, r.wo, ffn_loads, r.inner, r.act, r.slope, r.acc)
        ffn_finish(r.wide, r.acc, vec, r.out, 0)
        copies.store(r.out, out_out)
        g_load.wait()
        r.sums[...] = jnp.zeros_like(r.sums)
        ffn_back_start(r.g, r.acc, vec, r.inner, r.go, r.sums)
        copies.store(r.go, go_out)
        ffn_back(r.go, r.slope, r.wi, r.wo, [()] * BLOCKS, r.act, r.inner)
        attn_back_start(r.inner, r.before, vec, r.gb, r.sums)
        copies.store(r.gb, kept_out.at[4])
        r.gctx[...] = mm_nt(r.gb[...], r.w[3]).astype(BF16)
        attend_back(
            blocks, flags_s, flags_at, r.gctx, r.q, r.k, r.v, r.probs, r.gq, r.gk, r.gv
        )
        for i, source in enumerate((r.gq, r.gk, r.gv)):
            copies.store(source, kept_out.at[1 + i])
        r.gctx[...] = input_grad(r.before, r.gq, r.gk, r.gv, r.w)
        copies.store(r.gctx, grad_out)
        sum_rows(r.sums, r.extra, 11)
        copies.store(r.extra, extra_out)

    return run


def second_stage(
    control, word, cot_word, visual, cot_visual, flags, at_word, weights, blocks_w, blocks_v, name
):
    vecs, attn_w, inner_w, outer_w = weights
    width = word.shape[1]
    flat = [w for pair in attn_w for w in pair]
    scratch_w = section_scratch(word.shape[0], width, blocks_w)
    scratch_v = section_scratch(visual.shape[0], width, blocks_v)

    def body(first, block, ins, outs, scr, copies):
        word_in, cot_w_in, visual_in, cot_v_in, flags_in = ins[:5]
        weights_in = (ins[5:7], ins[7:15], ins[15:19])
        flags_s = scr[0]
        word_s = Refs(SECTION, scr[1 : 1 + len(scratch_w)])
        visual_s = Refs(SECTION, scr[1 + len(scratch_w) :])
        flags_load = [copies.load(flags_in, flags_s)]
        n_word = word_in.shape[0]
        pair = outs[1]
        n_visual = visual_in.shape[0]
        grad_out = outs[7]
        outs_w = (
            outs[0],
            pair.at[pl.ds(0, n_word)],
            pair.at[pl.ds(n_word, n_word)],
            grad_out.at[pl.ds(n_visual, n_word)],
            *outs[2:4],
        )
        outs_v = (*outs[4:7], grad_out.at[pl.ds(0, n_visual)], *outs[8:])
        run_w = section_round(
            first, word_s, word_in, cot_w_in, weights_in, flags_s, at_word, flags_load, blocks_w, copies, outs_w
        )
        run_v = section_round(
            jnp.logical_not(first), visual_s, visual_in, cot_v_in, weights_in, flags_s, 0, [], blocks_v, copies, outs_v
        )
        run_w()
        run_v()
        copies.drain()

    outs = []
    for piece, pairs in ((word, [2]), (visual, [1, 1])):
        rows = piece.shape[0]
        outs += [((rows, width), BF16)]
        outs += [((count * rows, width), BF16) for count in pairs]
        if piece is visual:
            outs += [((rows + word.shape[0], width), BF16)]
        outs += [((5, rows, width), BF16), ((16, width), F32)]
    inputs = [word, cot_word, visual, cot_visual, flags] + list(vecs) + flat
    inputs = inputs + list(inner_w) + list(outer_w)
    results = kernel_call(
        body,
        control,
        inputs,
        outs,
        [(flags.shape, F32)] + scratch_w + scratch_v,
        1 + 2 * (3 + 4 + 2 * BLOCKS) + 2 * 10,
        60,
        name,
    )
    return results[:4], results[4:]


def first_stage_back(
    control, grad, kept_1, ffn_0, flags, weights, blocks_1, buffer, name
):
    vecs, attn_w, inner_w, outer_w = weights
    slope_0, after_0 = ffn_0
    rows, width = after_0.shape
    total = kept_1[0].shape[0]
    n_word = total - rows
    flat = [w for pair in attn_w for w in pair]
    n_1 = len(blocks_1)
    narrow, wide = ((rows, width), BF16), ((rows, width), F32)
    tall, tall_wide = ((total, width), BF16), ((total, width), F32)
    hidden, square = ((BLOCKS, rows, width), BF16), ((4, width, width), BF16)

    def body(first, block, ins, outs, scr, copies):
        grad_in, rest = ins[0], ins[1:]
        kept_1_in, rest = rest[: 5 + n_1], rest[5 + n_1 :]
        (slope_in, after_in, flags_in), rest = rest[:3], rest[3:]
        vec_in, attn_in, ffn_in = rest[:2], rest[2:10], rest[10:14]
        kept_1_out, extra_1_out, word_out, go_out, gmid_out, extra_0_out = outs
        g1, q1, k1, v1, ctx1, before1, gb1, gctx1, gq1, gk1, gv1, flags_s = scr[:12]
        vec1, w1, sums1, extra1 = scr[12:16]
        vec0, wi, wo, slope, after, go, gi, acc, sums0, extra0 = scr[16:26]
        probs1 = scr[26:]
        other = jnp.logical_not(first)
        g_loads = [copies.load(grad_in, g1)]
        before_load = copies.load(kept_1_in[4], before1)
        vec1_load = copies.load_either(first, vec_in[0], vec_in[1], vec1)
        w1_load = copies.load_either(first, attn_in[6], attn_in[7], w1.at[3])
        flags_load = copies.load(flags_in, flags_s)
        loads1 = [copies.load(a, b) for a, b in zip(kept_1_in[:3], (q1, k1, v1))]
        loads1 += [copies.load(a, b) for a, b in zip(kept_1_in[5:], probs1)]
        w1_loads = [
            copies.load_either(first, attn_in[2 * i], attn_in[2 * i + 1], w1.at[i])
            for i in range(3)
        ]
        after_load = copies.load(after_in, after)
        vec0_load = copies.load_either(other, vec_in[0], vec_in[1], vec0)
        ffn_loads = load_ffn_weights(copies, other, ffn_in, wi, wo)
        slope_load = copies.load(slope_in, slope)
        for load in g_loads + [before_load, vec1_load]:
            load.wait()
        vec = vec1[...].astype(F32)
        sums1[...] = jnp.zeros_like(sums1)
        sums0[...] = jnp.zeros_like(sums0)
        attn_back_start(g1, before1, vec, gb1, sums1)
        copies.store(gb1, kept_1_out.at[4])
        w1_load.wait()
        gctx1[...] = mm_nt(gb1[...], w1[3]).astype(BF16)
        flags_load.wait()
        for load in loads1:
            load.wait()
        attend_back(blocks_1, flags_s, 0, gctx1, q1, k1, v1, probs1, gq1, gk1, gv1)
        for i, source in enumerate((gq1, gk1, gv1)):
            copies.store(source, kept_1_out.at[1 + i])
        for load in w1_loads:
            load.wait()
        gctx1[...] = input_grad(before1, gq1, gk1, gv1, w1)
        copies.store(gctx1.at[pl.ds(rows, n_word)], word_out)
        sum_rows(sums1, extra1, 11)
        copies.store(extra1, extra_1_out)
        after_load.wait()
        vec0_load.wait()
        vec = vec0[...].astype(F32)
        ffn_back_start(gctx1.at[pl.ds(0, rows)], after, vec, acc, go, sums0)
        copies.store(go, go_out)
        sum_rows(sums0, extra0, 11)
        copies.store(extra0, extra_0_out)
        slope_load.wait()
        for load in ffn_loads:
            load.wait()
        ffn_back(go, slope, wi, wo, [()] * BLOCKS, gi, acc)
        copies.store(acc, gmid_out)
        copies.drain()

    inputs = (
        [grad]
        + list(kept_1)
        + [slope_0, after_0, flags]
        + list(vecs)
        + flat
        + list(inner_w)
        + list(outer_w)
        + [buffer]
    )
    return kernel_call(
        body,
        control,
        inputs,
        [
            ((5, total, width), BF16),
            ((16, width), F32),
            ((n_word, width), BF16),
            narrow,
            wide,
            ((16, width), F32),
        ],
        [tall] * 5
        + [tall_wide]
        + [tall] * 5
        + [(flags.shape, F32), ((16, width), BF16), square, ((16, 8, width), F32), ((16, width), F32)]
        + [((16, width), BF16), square, square, hidden, wide, narrow, narrow, wide]
        + [((16, 8, width), F32), ((16, width), F32)]
        + probs_of(blocks_1),
        2 + 1 + 1 + 1 + 1 + 3 + n_1 + 3 + 1 + 1 + 2 * BLOCKS + 2 + 14,
        8,
        name,
        {len(inputs): 3},
    )


def first_section_back(control, gmid, kept, flags, weights, extra, blocks, name):
    vecs, attn_w, _, _ = weights
    rows, width = gmid.shape
    flat = [w for pair in attn_w for w in pair]
    n_b = len(blocks)
    narrow, wide = ((rows, width), BF16), ((rows, width), F32)

    def body(first, block, ins, outs, scr, copies):
        gmid_in, kept_in, rest = ins[0], ins[1 : 6 + n_b], ins[6 + n_b :]
        flags_in, extra_in, vec_in, attn_in = rest[0], rest[1], rest[2:4], rest[4:12]
        grad_out, kept_out, extra_out = outs
        g, q, k, v, before, gb, gctx, gq, gk, gv, flags_s, vec_s, w, sums, extra_s, more = scr[:16]
        probs = scr[16:]
        early = [copies.load(gmid_in, g), copies.load(kept_in[4], before)]
        early.append(copies.load_either(first, vec_in[0], vec_in[1], vec_s))
        wo_load = copies.load_either(first, attn_in[6], attn_in[7], w.at[3])
        loads = [copies.load(flags_in, flags_s), copies.load(extra_in, more)]
        loads += [copies.load(a, b) for a, b in zip(kept_in[:3], (q, k, v))]
        loads += [copies.load(a, b) for a, b in zip(kept_in[5:], probs)]
        w_loads = [
            copies.load_either(first, attn_in[2 * i], attn_in[2 * i + 1], w.at[i])
            for i in range(3)
        ]
        for load in early:
            load.wait()
        vec = vec_s[...].astype(F32)
        sums[...] = jnp.zeros_like(sums)
        attn_back_start(g, before, vec, gb, sums)
        copies.store(gb, kept_out.at[4])
        wo_load.wait()
        gctx[...] = mm_nt(gb[...], w[3]).astype(BF16)
        for load in loads:
            load.wait()
        attend_back(blocks, flags_s, 0, gctx, q, k, v, probs, gq, gk, gv)
        for i, source in enumerate((gq, gk, gv)):
            copies.store(source, kept_out.at[1 + i])
        sum_rows(sums, extra_s, 5)
        extra_s[...] += more[...]
        copies.store(extra_s, extra_out)
        for load in w_loads:
            load.wait()
        gctx[...] = input_grad(before, gq, gk, gv, w)
        copies.store(gctx, grad_out)
        copies.drain()

    return kernel_call(
        body,
        control,
        [gmid] + list(kept) + [flags, extra] + list(vecs) + flat,
        [narrow, ((5, rows, width), BF16), ((16, width), F32)],
        [wide, narrow, narrow, narrow, wide]
        + [narrow] * 5
        + [(flags.shape, F32), ((16, width), BF16), ((4, width, width), BF16)]
        + [((16, 8, width), F32), ((16, width), F32), ((16, width), F32)]
        + probs_of(blocks),
        3 + 1 + 2 + 3 + n_b + 3 + 6,
        0.01,
        name,
    )


def spare_rows(width):
    unit = 32 * lax.axis_size("dp")
    return -(4 * width + 16) % unit + 16


def attn_weight_grads(control, xs, ctx, kept, extra, buffers, name):
    rows, width = kept.shape[1:]
    n_x = len(xs)
    spare = spare_rows(width)
    total = 4 * width + spare
    half = total // 2
    narrow = ((rows, width), BF16)

    def body(first, block, ins, outs, scr, copies):
        x_in, (kept_in, extra_in) = ins[:n_x], ins[n_x : n_x + 2]
        ctx_in = kept_in.at[0] if ctx is None else ins[n_x + 2]
        x_s, ctx_s, gq_s, gk_s, gv_s, gb_s, extra_s, gw_s, sums_s = scr
        at, x_loads = 0, []
        for piece in x_in:
            x_loads.append(copies.load(piece, x_s.at[pl.ds(at, piece.shape[0])]))
            at += piece.shape[0]
        loads = [copies.load(kept_in.at[1 + i], b) for i, b in enumerate((gq_s, gk_s, gv_s, gb_s))]
        ctx_load = copies.load(ctx_in, ctx_s)
        extra_load = copies.load(extra_in, extra_s)
        for load in x_loads:
            load.wait()
        for i, (left, right) in enumerate(((x_s, gq_s), (x_s, gk_s), (x_s, gv_s), (ctx_s, gb_s))):
            loads[i].wait()
            if i == 3:
                ctx_load.wait()
            gw_s[pl.ds(i * width, width), :] = mm_tn(left[...], right[...]).astype(BF16)
        sums_s[...] = jnp.zeros_like(sums_s)

        def bias_sums(where):
            sums_s[0] += folded(gq_s[where, :].astype(F32))
            sums_s[1] += folded(gv_s[where, :].astype(F32))

        each_rows(rows, 32, bias_sums)
        extra_load.wait()
        for i in range(2):
            extra_s[i : i + 1, :] = jnp.sum(sums_s[i], 0, keepdims=True)
        tail = jnp.concatenate([extra_s[...], jnp.zeros((spare - 16, width), F32)], 0)
        gw_s[pl.ds(4 * width, spare), :] = tail.astype(BF16)
        lower = lax.rem(block, 2) == 0
        keep_out, send_out = outs
        copies.store_either(lower, gw_s.at[pl.ds(0, half)], keep_out, send_out)
        copies.store_either(lower, gw_s.at[pl.ds(half, half)], send_out, keep_out)
        copies.drain()

    inputs = list(xs) + [kept, extra] + ([] if ctx is None else [ctx])
    aliases = {}
    if buffers is not None:
        aliases = {len(inputs) + 1: 0, len(inputs) + 2: 1}
        inputs = inputs + list(buffers)
    return kernel_call(
        body,
        control,
        inputs,
        [((half, width), BF16)] * 2,
        [narrow] * 6
        + [((16, width), F32), ((total, width), BF16), ((2, 8, width), F32)],
        n_x + 4 + 2 + 2,
        2,
        name,
        aliases,
    )


def assemble_ffn(control, evens, odds, name):
    rows, width = evens[0][0].shape

    def body(first, block, ins, outs, scr, copies, core, unused):
        groups = (ins[: 2 * BLOCKS], ins[2 * BLOCKS :])
        inner_out, outer_out, bias_out = outs
        own_s, far_s, out_s, bias_s = scr

        def fetch(j):
            slot, waits = j % 2, []
            for k, target in ((0, own_s), (1, far_s)):
                mine = groups[0][2 * j + k]
                waits.append(
                    copies.load_either(core == 0, mine, groups[1][2 * j + k], target.at[slot])
                )
            return waits

        loads = {0: fetch(0)}
        pending = []
        for j in range(BLOCKS):
            if j + 1 < BLOCKS:
                loads[j + 1] = fetch(j + 1)
            for load in loads[j]:
                load.wait()
            if j >= 2:
                for copy in pending[j - 2]:
                    copy.wait()
            slot = j % 2

            def turn(where):
                value = own_s[slot, where, :].astype(F32) + far_s[slot, where, :].astype(F32)
                out_s[slot, where, :] = jnp.where(unused == 1, 0.0, value)

            each_rows(rows, 32, turn)
            bias_s[j : j + 1, :] = out_s[slot, 2 * width : 2 * width + 1, :]
            part = pl.ds(j * width, width)
            pending.append(
                [
                    copies.store(out_s.at[slot, pl.ds(0, width)], inner_out.at[:, part], True),
                    copies.store(out_s.at[slot, pl.ds(width, width)], outer_out.at[part, :], True),
                ]
            )
        bias = copies.store(bias_s, bias_out, True)
        for copy in pending[-2] + pending[-1] + [bias]:
            copy.wait()

    return kernel_call(
        body,
        control,
        [piece for pair in evens for piece in pair] + [piece for pair in odds for piece in pair],
        [
            ((width, BLOCKS * width), F32),
            ((BLOCKS * width, width), F32),
            ((8, width), F32),
        ],
        [((2, rows, width), BF16)] * 2 + [((2, rows, width), F32), ((8, width), F32)],
        4 * BLOCKS + 1,
        0.01,
        name,
        more=2,
    )


def assemble_attn(control, even, odd, name):
    half, width = even[0].shape
    spare = spare_rows(width)

    def body(first, block, ins, outs, scr, copies, core, unused):
        in_s, out_s = scr
        loads = []
        for h in (0, 1):
            sem = copies.next_sem()
            for p, group in enumerate((ins[:2], ins[2:4])):
                source = group[0 if h == p else 1]

                @pl.when(core == p)
                def _(source=source):
                    pltpu.make_async_copy(source, in_s.at[pl.ds(h * half, half)], sem).start()

            loads.append(pltpu.make_async_copy(ins[0], in_s.at[pl.ds(h * half, half)], sem))

        def turn(where):
            out_s[where, :] = in_s[where, :].astype(F32)

        pieces = [(i * width, width) for i in range(4)] + [(4 * width, spare)]
        waited = 0
        for i, (at, size) in enumerate(pieces):
            while waited < 2 and waited * half < at + size:
                loads[waited].wait()
                waited += 1

            def shifted(where, at=at):
                turn(pl.ds(pl.multiple_of(at + where.start, 32), where.size))

            each_rows(size, 32, shifted)
            copies.store(out_s.at[pl.ds(at, size)], outs[i])
        copies.drain()

    total = 4 * width + spare
    return kernel_call(
        body,
        control,
        list(even) + list(odd),
        [((width, width), F32)] * 4 + [((spare, width), F32)],
        [((total, width), BF16), ((total, width), F32)],
        2 + 5,
        7,
        name,
        more=2,
    )


def ffn_weight_grads(
    control, mids, gos, which, group, vecs, w_inner, w_outer, name, others, first_piece
):
    rows, width = mids[0][1], w_inner[0].shape[0]
    count, n_j = len(mids), len(which)
    together = rows * group
    wide = ((together, width), F32)
    tall = ((count * rows, width), BF16)
    arrays = [array for array, _, _ in mids] + [array for array, _, _ in gos]
    n_others = len(others)
    starts = [start for _, _, start in mids] + [start for _, _, start in gos]

    def body(first, block, ins, outs, scr, copies, early, place):
        vec_a, vec_b, wi_a, wi_b, wo_a, wo_b = ins[2 * count : 2 * count + 6]
        others_in = ins[2 * count + 6 :]
        mid_s, go_s, gi_s, act_s, vec_s, wi_s, wo_s, inner_s, back_s, gw_s, sums_s = scr
        vec_load = copies.load_either(first, vec_a, vec_b, vec_s)
        w_loads = []
        for at, j in enumerate(which):
            part = pl.ds(j * width, width)
            w_loads.append(copies.load_either(first, wi_a.at[:, part], wi_b.at[:, part], wi_s.at[at]))
            w_loads.append(copies.load_either(first, wo_a.at[part, :], wo_b.at[part, :], wo_s.at[at]))
        base = copies.used
        for i in range(count):
            piece = first_piece + i
            slot = jnp.where(early == 1, i, i ^ lax.rem(place, GROUP))
            owner = jnp.where(early == 1, piece, piece ^ place)
            spot = pl.ds(pl.multiple_of(slot * rows, 32), rows)
            mid_sem, go_sem = copies.sems.at[base + slot], copies.sems.at[base + count + slot]
            source = ins[i].at[pl.ds(starts[i], rows)]
            if n_others:

                @pl.when(early == 1)
                def _(source=source, spot=spot, sem=mid_sem):
                    pltpu.make_async_copy(source, mid_s.at[spot], sem).start()

                @pl.when(early != 1)
                def _(source=others_in[i], spot=spot, sem=mid_sem):
                    pltpu.make_async_copy(source, mid_s.at[spot], sem).start()

                at = pl.multiple_of(owner * rows, 32)
            else:
                pltpu.make_async_copy(source, mid_s.at[spot], mid_sem).start()
                at = starts[count + i]
            source = ins[count + i].at[pl.ds(at, rows)]
            pltpu.make_async_copy(source, go_s.at[spot], go_sem).start()

        def wait_for(i):
            spot = pl.ds(i * rows, rows)
            for k, target in enumerate((mid_s, go_s)):
                source, sem = ins[0].at[pl.ds(0, rows)], copies.sems.at[base + k * count + i]
                pltpu.make_async_copy(source, target.at[spot], sem).wait()

        copies.used += 2 * count
        vec_load.wait()
        for at, j in enumerate(which):
            w_loads[2 * at].wait()
            w_loads[2 * at + 1].wait()
            bias = vec_s[8 + j : 9 + j, :].astype(F32)
            sums_s[...] = jnp.zeros_like(sums_s)
            for i in range(count // group):
                if at == 0:
                    for k in range(group * i, group * (i + 1)):
                        wait_for(k)
                spot = slice(i * together, (i + 1) * together)
                inner_s[...] = mm(mid_s[spot, :], wi_s[at])
                back_s[...] = mm_nt(go_s[spot, :], wo_s[at])

                def turn(where, base=i * together):
                    inner = inner_s[where, :] + bias
                    phi = 0.5 * (1.0 + lax.erf(inner * (0.5**0.5)))
                    density = jnp.exp(-0.5 * inner * inner) * 0.3989422804014327
                    target = pl.ds(pl.multiple_of(base + where.start, 32), where.size)
                    act_s[target, :] = (inner * phi).astype(BF16)
                    rounded = (back_s[where, :] * (phi + inner * density)).astype(BF16)
                    gi_s[target, :] = rounded
                    sums_s[...] += folded(rounded.astype(F32))

                each_rows(together, 32, turn)
            out, gw = outs[at], gw_s.at[at]
            gw[pl.ds(0, width), :] = mm_tn(mid_s[...], gi_s[...]).astype(BF16)
            copies.store(gw.at[pl.ds(0, width)], out.at[pl.ds(0, width)])
            gw[pl.ds(width, width), :] = mm_tn(act_s[...], go_s[...]).astype(BF16)
            tail = jnp.concatenate(
                [jnp.sum(sums_s[...], 0, keepdims=True), jnp.zeros((EXTRA - 1, width), F32)], 0
            )
            gw[pl.ds(2 * width, EXTRA), :] = tail.astype(BF16)
            copies.store(gw.at[pl.ds(width, width + EXTRA)], out.at[pl.ds(width, width + EXTRA)])
        copies.drain()

    square = ((n_j, width, width), BF16)
    return kernel_call(
        body,
        control,
        arrays + list(vecs) + list(w_inner) + list(w_outer) + list(others),
        [((2 * width + EXTRA, width), BF16)] * n_j,
        [
            tall,
            tall,
            tall,
            tall,
            ((16, width), BF16),
            square,
            square,
            wide,
            wide,
            ((n_j, 2 * width + EXTRA, width), BF16),
            ((8, width), F32),
        ],
        1 + 4 * n_j + 2 * count,
        0.01,
        name,
        more=2,
    )


def swapper(sections):
    n = lax.axis_size("dp")

    def swap(value, bit):
        pairs = [(s * n + i, s * n + (i ^ bit)) for s in sections for i in range(n)]
        return lax.ppermute(value, ("section", "dp"), pairs)

    return swap


def fold(control, parts, cuts, name):
    rows, width = parts[0].shape
    piece = rows // cuts
    n_parts = len(parts)

    def body(first, kept, ins, outs, scr, copies):
        total, more = scr[0], scr[1:]
        loads = [copies.load(a, b) for a, b in zip(ins, scr)]
        for load in loads:
            load.wait()

        def add(where):
            value = total[where, :].astype(F32)
            for other in more:
                value = value + other[where, :].astype(F32)
            total[where, :] = value.astype(BF16)

        each_rows(rows, 16, add)
        for i in list(range(1, cuts)) + [0]:
            at = pl.multiple_of((kept ^ i) * piece, 16) if cuts > 1 else 0
            copies.store(total.at[pl.ds(at, piece)], outs[i])
        copies.drain()

    shape = ((rows, width), BF16)
    outs = [((piece, width), BF16)] * cuts
    return kernel_call(body, control, parts, outs, [shape] * n_parts, n_parts + cuts, 0.01, name)


def join(control, parts, name):
    rows, width = parts[0].shape

    def body(first, own, ins, outs, scr, copies):
        loads = []
        for i, source in enumerate(ins):
            spot = pl.ds(pl.multiple_of((own ^ i) * rows, 16), rows)
            loads.append(copies.load(source, scr[0].at[spot]))
        for load in loads:
            load.wait()
        copies.store(scr[0], outs[0])
        copies.drain()

    whole = ((len(parts) * rows, width), BF16)
    return kernel_call(body, control, parts, [whole], [whole], len(parts) + 1, 0.01, name)[0]


def tied(value, *others):
    return lax.optimization_barrier((value, others))[0]


def per_device(
    tokens,
    cotangent,
    task_flags,
    w_query,
    w_key,
    w_value,
    w_attn_out,
    b_query,
    b_value,
    b_attn_out,
    norm1_gain,
    norm1_bias,
    w_inner,
    b_inner,
    w_outer,
    b_outer,
    norm2_gain,
    norm2_bias,
):
    section = lax.axis_index("section")
    stage, core = section // 2, section % 2
    items, seq_len, width = tokens.shape
    words = seq_len - OBJ
    n_visual, n_word = items * OBJ, items * words
    is_first = stage == 0

    def swap_stage(value):
        return lax.ppermute(value, "section", [(0, 2), (1, 3), (2, 0), (3, 1)])

    def swap_core(value):
        return lax.ppermute(value, "section", [(0, 1), (1, 0), (2, 3), (3, 2)])

    flags_far = swap_stage(task_flags)
    tokens_far = swap_stage(tokens)
    attn_w = [w[0] for w in (w_query, w_key, w_value, w_attn_out)]
    vec = jnp.concatenate(
        [
            b_query,
            b_value,
            b_attn_out,
            norm1_gain,
            norm1_bias,
            b_outer,
            norm2_gain,
            norm2_bias,
            b_inner.reshape(BLOCKS, width),
            jnp.zeros((4, width), BF16),
        ],
        0,
    )
    vecs = (vec, swap_core(vec))
    attn_w = [(w, swap_core(w)) for w in attn_w]
    inner_w = (w_inner[0], swap_core(w_inner[0]))
    outer_w = (w_outer[0], swap_core(w_outer[0]))
    cot_far = swap_stage(cotangent)

    flags = task_flags.astype(F32)
    far = flags_far.astype(F32)
    flags = jnp.where(
        is_first, jnp.concatenate([flags, far]), jnp.concatenate([far, flags])
    )
    every = jnp.concatenate([jnp.repeat(flags, OBJ), jnp.repeat(flags, words)])
    flags = jnp.broadcast_to(every[:, None], (every.shape[0], LANES))

    def split(first, second):
        visual = jnp.concatenate([first[:, :OBJ], second[:, :OBJ]], 0)
        word = jnp.concatenate([first[:, OBJ:], second[:, OBJ:]], 0)
        return visual.reshape(2 * n_visual, width), word.reshape(2 * n_word, width)

    place = lax.axis_index("dp")
    side = place % 2
    block = 2 * side + core

    order = []

    def control(at, parity):
        return Control([stage == at, core == parity, block], order)

    even_0, odd_0, even_1, odd_1 = control(0, 0), control(0, 1), control(1, 0), control(1, 1)
    even_any = Control([core >= 0, core == 0, block, stage == 0, place], order)
    odd_late = Control([stage == 1, core == 1, block, stage < 0, place], order)
    blocks_v = [(g * n_visual, n_visual, OBJ, g * n_visual, n_visual, OBJ) for g in (0, 1)]
    blocks_w = [(g * n_word, n_word, words, g * n_word, n_word, words) for g in (0, 1)]
    blocks_x = []
    for g in (0, 1):
        v_at, w_at = g * n_visual, 2 * n_visual + g * n_word
        blocks_x.append((v_at, n_visual, OBJ, w_at, n_word, words))
        blocks_x.append((w_at, n_word, words, v_at, n_visual, OBJ))

    visual_0, word_0 = split(tokens, tokens_far)
    grad_v4, grad_w4 = split(cot_far, cotangent)
    ffn_w = (vecs, inner_w, outer_w)
    weights = (vecs, attn_w, inner_w, outer_w)
    at_word = 2 * n_visual

    kept_0, mid_0, ffn_0, visual_1, kept_1, visual_2, word_2 = first_stage_forward(
        even_0, visual_0, word_0, flags, weights, blocks_v, blocks_x, "s01_f"
    )
    swap_all, swap_early, swap_late = swapper(range(4)), swapper((0, 1)), swapper((2, 3))
    line = []
    while 2 ** (len(line) + 1) < lax.axis_size("dp"):
        line.append(2 ** (len(line) + 1))
    by_size = [2**i for i in reversed(range(len(line) + 1))]
    side_early = by_size[:1] + [1] + by_size[1:-1]

    def spread(value, swap, bits):
        pieces = [value]
        for mask in range(1, lax.axis_size("dp")):
            bit = [bit for bit in bits if mask & bit][-1]
            pieces.append((mask, bit))
        for turn in range(1, len(bits) + 1):
            for mask in range(1, len(pieces)):
                if bin(mask).count("1") == turn:
                    bit = pieces[mask][1]
                    pieces[mask] = swap(pieces[mask ^ bit], bit)
        return pieces

    def turn_of(pieces, turn):
        return [piece for mask, piece in enumerate(pieces) if bin(mask).count("1") == turn]

    def held(pieces, turn, value):
        value, now = lax.optimization_barrier((value, turn_of(pieces, turn)))
        now = iter(now)
        return value, [
            next(now) if bin(mask).count("1") == turn else piece
            for mask, piece in enumerate(pieces)
        ]

    def items_of(visual, word):
        return jnp.concatenate(
            [visual.reshape(items, OBJ, width), word.reshape(items, words, width)], 1
        )

    word_2, visual_2 = swap_stage(word_2), swap_stage(visual_2)
    mids_0 = lax.all_gather(mid_0, "dp", axis=0, tiled=True)
    of_word, of_visual = second_stage(
        odd_1,
        word_2,
        grad_w4,
        visual_2,
        grad_v4,
        flags,
        at_word,
        weights,
        blocks_w,
        blocks_v,
        "s23",
    )
    word_4, pair_3, kept_3, extra_3 = of_word
    visual_4, mid_2, go_2, grad_2, kept_2, extra_2 = of_visual
    pairs = spread(pair_3, swap_late, by_size)
    mids_2 = spread(mid_2, swap_late, side_early)
    grad_2, order[0] = lax.optimization_barrier((swap_stage(grad_2), order[0]))
    odd_c = attn_weight_grads(odd_1, [word_2], None, kept_3, extra_3, None, "s3_attn_w")
    even_c = attn_weight_grads(even_1, [visual_2], None, kept_2, extra_2, None, "s2_attn_w")
    order[0], pairs = held(pairs, 1, order[0])
    rows_v, rows_w = 2 * n_visual, 2 * n_word
    blocks = {"odd": [], "even": []}

    def multiply(key, which):
        if key == "odd":
            block_mids = [(piece, rows_w, 0) for piece in pairs]
            block_gos = [(piece, rows_w, rows_w) for piece in pairs]
        else:
            count = lax.axis_size("dp")
            block_mids = [(mids_0, rows_v, i * rows_v) for i in range(count)]
            block_gos = [(gos, rows_v, i * rows_v) for i in range(count)]
        control, group = (odd_late, 2) if key == "odd" else (even_any, 2)
        name = f"{key}_ffn_w{which[0]}"
        others = mids_2 if key == "even" else ()
        results = None
        for at in range(0, len(block_mids), GROUP):
            some = slice(at, at + GROUP)
            more = ffn_weight_grads(
                control, block_mids[some], block_gos[some], which, group, *ffn_w, name, others[some], at
            )
            results = [a + b for a, b in zip(results, more)] if results else more
        for result in results:
            blocks[key].append((result, swap_core(result)))

    visual_4, grad_2 = lax.optimization_barrier((visual_4, grad_2))
    mixed_own = items_of(visual_4[n_visual:], word_4[n_word:])
    mixed_far = items_of(visual_4[:n_visual], word_4[:n_word])
    back_1, extra_1, grad_w0, go_even, gmid_0, extra_0 = first_stage_back(
        odd_0, grad_2, kept_1, ffn_0, flags, weights, blocks_x, go_2, "s10_b"
    )
    gos = lax.all_gather(go_even, "dp", axis=0, tiled=True)
    order[0], pairs = held(pairs, 2, order[0])
    order[0], mids_2 = held(mids_2, 1, order[0])
    order[0], mids_0 = lax.optimization_barrier((order[0], mids_0))
    odd_c = attn_weight_grads(
        odd_0, [visual_1, word_0], kept_1[3], back_1, extra_1, odd_c, "s1_attn_w"
    )
    odd_c_core = swap_core(odd_c[1])
    n_line = lax.axis_size("dp") // 2
    far_side = place // 2
    at_side = Control([core >= 0, core >= 0, side], order)
    at_line = Control([core >= 0, core >= 0, far_side], order)

    def chain(key, keep, core_far):
        kept, sent = fold(at_side, [keep, core_far], 2, f"{key}_fold_core")
        far = swap_all(sent, 1)
        yield
        kept, *sent = fold(at_line, [kept, far], n_line, f"{key}_fold_side")
        far = [swap_all(part, 2 * (i + 1)) for i, part in enumerate(sent)]
        yield
        kept = fold(at_line, [kept] + far, 1, f"{key}_fold_line")[0]
        far = [swap_all(kept, 2 * (i + 1)) for i in range(n_line - 1)]
        yield
        kept = join(at_line, [kept] + far, f"{key}_join_line")
        far = swap_all(kept, 1)
        yield
        yield join(at_side, [kept, far], f"{key}_join_side")

    chains = {"co": chain("odd", odd_c[0], odd_c_core)}
    next(chains["co"])
    grad_v0, back_0, extra_0 = first_section_back(
        even_0, gmid_0, kept_0, flags, weights, extra_0, blocks_v, "s0_b"
    )
    order[0], pairs = held(pairs, 3, order[0])
    multiply("odd", (0, 1))
    even_c = attn_weight_grads(
        even_0, [visual_0], kept_0[3], back_0, extra_0, even_c, "s0_attn_w"
    )
    chains["ce"] = chain("even", even_c[0], swap_core(even_c[1]))
    multiply("odd", (2, 3))
    control_end = Control([core >= 0, core >= 0, block, core, section == 1], order)
    ffn_out, far_grad = None, None
    sums = {}
    for item in PLAN:
        if item in chains:
            sums[item] = next(chains[item])
        elif item[0] == "m":
            order[0], mids_2 = held(mids_2, int(item[1]), order[0])
        elif item == "end":
            grad_far = items_of(grad_v0[n_visual:], grad_w0[n_word:])
            mixed_far, grad_far, order[0] = lax.optimization_barrier(
                (mixed_far, grad_far, order[0])
            )
            mixed_far, grad_far = swap_stage(mixed_far), swap_stage(grad_far)
            odd_c_far = swap_core(sums["co"])
            ffn_out = assemble_ffn(control_end, blocks["even"], blocks["odd"], "ffn_out")
            order[0], mixed_far, grad_far, odd_c_far = lax.optimization_barrier(
                (order[0], mixed_far, grad_far, odd_c_far)
            )
        else:
            multiply("even", tuple(int(j) for j in item[1:]))
    grad_inner, grad_outer, inner_bias = ffn_out
    odd_c, even_c = sums["co"], sums["ce"]
    *square, small = assemble_attn(
        control_end, [even_c, swap_core(even_c)], [odd_c, odd_c_far], "attn_out"
    )
    mixed = jnp.where(is_first, mixed_far, mixed_own)
    tokens_grad = jnp.where(is_first, items_of(grad_v0[:n_visual], grad_w0[:n_word]), grad_far)
    return (
        mixed,
        tokens_grad,
        square[0][None],
        square[1][None],
        square[2][None],
        square[3][None],
        small[0:1],
        small[1:2],
        small[2:3],
        small[3:4],
        small[4:5],
        grad_inner[None],
        inner_bias[:BLOCKS].reshape(1, BLOCKS * width),
        grad_outer[None],
        small[10:11],
        small[8:9],
        small[9:10],
    )


def solution(mesh):
    tokens = P(("section", "dp"), None, None)
    matrix = P("section", None, None)
    vector = P("section", None)
    placed = (
        (tokens, tokens, P(("section", "dp")))
        + (matrix,) * 4
        + (vector,) * 5
        + (matrix, vector, matrix)
        + (vector,) * 3
    )
    return jax.shard_map(
        per_device,
        mesh=mesh,
        in_specs=placed,
        out_specs=(tokens, tokens)
        + (matrix,) * 4
        + (vector,) * 5
        + (matrix, vector, matrix)
        + (vector,) * 3,
        check_vma=False,
    )
```
